256 devices in a mesh: col: 32 (over z, x_lo, core), row: 8 (over y, x_hi).
Axes of the slice: x: 4 (x_hi: 2, x_lo: 2; x = x_hi * 2 + x_lo), y: 4, z: 8, core: 2. Of those that a mesh axis runs over, the one named last changes fastest.
Arguments:
- inputs: bfloat16 [1024, 8192], P('col', 'row'), may hold values from -6 to 6
- weight: bfloat16 [8192, 28672], P('row', 'col'), may hold values from -0.0625 to 0.0625
- adapter_down_factors: bfloat16 [16, 16, 8192], P(None, None, 'row'), may hold values from -0.06629126 to 0.06629126
- adapter_up_factors: bfloat16 [16, 16, 28672], P(None, None, 'col'), may hold values from -1.5 to 1.5
- magnitude: float32 [16, 28672], P(None, 'col'), may hold values from 0.5 to 2
- cotangent: bfloat16 [1024, 28672], P('row', 'col'), may hold values from -6 to 6
- tenant: int32 [1024], replicated, may hold values from 0 to 15, as said below
Outputs:
- output: bfloat16 [1024, 28672], P('row', 'col')
- grad_inputs: bfloat16 [1024, 8192], P('col', 'row')
- grad_b: float32 [16, 16, 28672], P(None, None, 'col')
- grad_m: float32 [16, 28672], P(None, 'col')
The draws below stay inside these ranges and needn't reach their ends.
Inputs may be any that keep to these rules, and one draw needn't show every extreme that they name: `tenant`: constant on each aligned block of 128 tokens; both 0 and 15 occur in every draw.
All inputs are finite; a program needn't handle non-finite values.
Results may differ from the reference program's by a relative error of at most 0.0051.
Values may be sent and summed in bfloat16 or wider, within the bound.
A program may use at most 128 MiB of HBM per device.

```python
import math
import jax
import jax.numpy as jnp
from jax import lax

MODEL_WIDTH = 8192
HIDDEN_UNITS = 28672
TENANT_COUNT = 16
ADAPTER_RANK = 16
BLOCK = 128
TOKENS = 1024


def draw_tenant(key, part):
    key = jax.random.fold_in(key, 7)
    nblocks = TOKENS // BLOCK
    first, second = jax.random.split(key)
    block_tenant_index = jax.random.randint(first, (nblocks,), 0, TENANT_COUNT)
    where_top = jax.random.randint(second, (), 0, nblocks)
    places = jnp.arange(nblocks)
    block_tenant_index = jnp.where(places == where_top, TENANT_COUNT - 1, block_tenant_index)
    block_tenant_index = jnp.where(places == (where_top + 1) % nblocks, 0, block_tenant_index)
    return jnp.repeat(block_tenant_index, BLOCK).astype(jnp.int32)


def combine_factors(common, own, strength, sign_key):
    signs = jax.random.randint(sign_key, (TENANT_COUNT, ADAPTER_RANK, 1), 0, 2).astype(jnp.float32) * 2.0 - 1.0
    loading = strength * signs
    mixed = loading * common + jnp.sqrt(1.0 - loading * loading) * own
    return mixed * float(MODEL_WIDTH) ** (-0.5)


def draw_adapter_down_factors(key, part):
    key = jax.random.fold_in(key, 11)
    first, second, third, fourth = jax.random.split(key, 4)
    common = jnp.clip(jax.random.normal(first, (TENANT_COUNT, 1, MODEL_WIDTH), jnp.float32), -4.0, 4.0)
    own = jnp.clip(jax.random.normal(second, (TENANT_COUNT, ADAPTER_RANK, MODEL_WIDTH), jnp.float32), -4.0, 4.0)
    strength = jax.random.uniform(third, (TENANT_COUNT, 1, 1), jnp.float32, 0.5, 0.8)
    return combine_factors(common, own, strength, fourth).astype(jnp.bfloat16)


def spiked(array, rng, source, target, shards_of, factor):
    owner, partner = [(jnp.arange(array.shape[axis_at]) // (array.shape[axis_at] // shards_of)).reshape([-1 if axis == axis_at else 1 for axis in range(array.ndim)]) for axis_at in (source, target)]
    chosen = jax.random.permutation(rng, shards_of)[partner]
    strong = (owner == chosen) | (owner == (partner + shards_of // 2) % shards_of)
    return jnp.where(strong, factor * array, array)


def shard_levels(stream_key, extent, pieces, least, high):
    level, own = 1.0, jax.random.fold_in(stream_key, 6)
    for position, parts in pieces:
        draws = jnp.exp(jax.random.uniform(jax.random.fold_in(own, position), (parts,), jnp.float32, least / len(pieces), high / len(pieces)))
        level = level * jnp.repeat(draws, extent[position] // parts).reshape([-1 if axis == position else 1 for axis in range(len(extent))])
    return level


def centred(stream_key, dims, spread, most, cuts=(), kind=jnp.bfloat16):
    values = jax.random.normal(stream_key, dims, jnp.float32) * spread
    if len(cuts) > 0:
        values = shard_levels(stream_key, dims, cuts, -0.22, 0.18) * values
    return jnp.clip(values, min=-most, max=most).astype(kind)


def gaussian_with(stream_key, extent, spread, reach, cuts, heavy, held_as=jnp.bfloat16):
    entries = spread * jax.random.normal(stream_key, extent, jnp.float32)
    if cuts:
        entries = entries * shard_levels(stream_key, extent, cuts, -0.22, 0.18)
    return jnp.clip(spiked(entries, jax.random.fold_in(stream_key, 3), *heavy), -reach, reach).astype(held_as)


def setup_inputs(seed: int = 0) -> dict:
    arg_keys = jax.random.split(jax.random.key(seed), 8)
    inputs = centred(arg_keys[0], (TOKENS, MODEL_WIDTH), 1.0, 6.0, ((0, 32), (1, 8)))
    weight = centred(arg_keys[1], (MODEL_WIDTH, HIDDEN_UNITS), MODEL_WIDTH ** -0.5, 0.0625, ((0, 8), (1, 32)))
    adapter_down_factors = draw_adapter_down_factors(jax.random.fold_in(arg_keys[7], 71), 0)
    adapter_up_factors = centred(arg_keys[3], (TENANT_COUNT, ADAPTER_RANK, HIDDEN_UNITS), ADAPTER_RANK ** -0.5, 1.5, ((2, 32),))
    magnitude = jnp.clip(jnp.exp(math.log(2.0) - 1.3862944 * jax.random.uniform(arg_keys[4], (TENANT_COUNT, HIDDEN_UNITS), jnp.float32) ** shard_levels(arg_keys[4], (TENANT_COUNT, HIDDEN_UNITS), ((1, 32),), -0.2, 0.2)), 0.5, 2.0)
    cotangent = gaussian_with(arg_keys[5], (TOKENS, HIDDEN_UNITS), 1.0, 6.0, ((0, 8), (1, 32)), (1, 0, 32, 2.75))
    tenant = draw_tenant(jax.random.fold_in(arg_keys[7], 71), 0)
    return {"inputs": inputs, "weight": weight, "adapter_down_factors": adapter_down_factors, "adapter_up_factors": adapter_up_factors, "magnitude": magnitude, "cotangent": cotangent, "tenant": tenant}


HIGH = lax.Precision.HIGHEST
EPS = 1e-06

def squared_column_norms(weight, adapter_down_factors, adapter_up_factors):
    tenant_number, rank_dimension, width_dimension = adapter_down_factors.shape
    wf = weight.astype(jnp.float32)
    wsq = lax.optimization_barrier(jnp.sum(wf * wf, axis=0))
    cross_product_term = jnp.dot(adapter_down_factors.reshape(tenant_number * rank_dimension, width_dimension), weight, preferred_element_type=jnp.float32).reshape(tenant_number, rank_dimension, -1)
    down_flat_view = adapter_down_factors.astype(jnp.float32)
    up_flat_view = adapter_up_factors.astype(jnp.float32)
    gram = jnp.einsum('trd,tsd->trs', down_flat_view, down_flat_view, precision=HIGH)
    quad = jnp.einsum('trj,trs,tsj->tj', up_flat_view, gram, up_flat_view, precision=HIGH)
    return wsq[None, :] + 2.0 * lax.optimization_barrier(jnp.sum(cross_product_term * up_flat_view, axis=1)) + quad

def reference(inputs, weight, adapter_down_factors, adapter_up_factors, magnitude, cotangent, tenant):
    tenant_number, rank_dimension, width_dimension = adapter_down_factors.shape
    onehot = (tenant[:, None] == jnp.arange(tenant_number, dtype=jnp.int32)[None, :]).astype(jnp.float32)
    mask = jnp.repeat(onehot, rank_dimension, axis=1)
    down_factor_flat = adapter_down_factors.reshape(tenant_number * rank_dimension, width_dimension)
    up_factor_flat = adapter_up_factors.reshape(tenant_number * rank_dimension, -1)
    contract = (((1,), (1,)), ((), ()))
    low_all = lax.dot_general(inputs, down_factor_flat, contract, preferred_element_type=jnp.float32)
    low_wide = (low_all * mask).astype(jnp.bfloat16)
    pre = jnp.dot(inputs, weight, preferred_element_type=jnp.float32) + jnp.dot(low_wide, up_factor_flat, preferred_element_type=jnp.float32)
    norm_squared_total = squared_column_norms(weight, adapter_down_factors, adapter_up_factors)
    scale = magnitude / jnp.sqrt(norm_squared_total + EPS)
    token_scale = jnp.dot(onehot, scale, precision=HIGH)
    output = (token_scale * pre).astype(jnp.bfloat16)
    gradient_scaled = (cotangent.astype(jnp.float32) * token_scale).astype(jnp.bfloat16)
    grad_b = jnp.dot(low_wide.T, gradient_scaled, preferred_element_type=jnp.float32).reshape(tenant_number, rank_dimension, -1)
    back_wide = lax.dot_general(gradient_scaled, up_factor_flat, contract, preferred_element_type=jnp.float32) * mask
    grad_inputs = lax.dot_general(gradient_scaled, weight, contract, preferred_element_type=jnp.float32)
    grad_inputs = grad_inputs + jnp.dot(back_wide, down_factor_flat.astype(jnp.float32), precision=HIGH)
    grad_inputs = grad_inputs.astype(jnp.bfloat16)
    product = cotangent.astype(jnp.float32) * output.astype(jnp.float32)
    grad_m = jnp.dot(onehot.T, product, precision=HIGH) / magnitude
    return (output, grad_inputs, grad_b, grad_m)
```

```python
import functools

import jax
import jax.numpy as jnp
from jax import lax
from jax.experimental import pallas as pl
from jax.experimental.pallas import tpu as pltpu
from jax.sharding import PartitionSpec as P

EPS = 1e-06
MESH = pl.DeviceIdType.MESH
BF = jnp.bfloat16
F32 = jnp.float32

NZ, NY, NR = 8, 4, 8
FIRST_BACK = 6
STEPS = FIRST_BACK + NZ + 2


def mm(a, b):
    return jnp.dot(a, b, preferred_element_type=F32)


def mm_nt(a, b):
    return lax.dot_general(a, b, (((1,), (1,)), ((), ())), preferred_element_type=F32)


def lane_tiles(width):
    return [(n, min(n + 256, width)) for n in range(0, width, 256)]


def kernel(
    ten, x_in, w_in, a_in, u_in, mag, c_in,
    out_ref, gi_ref, gb_ref, gm_ref,
    w_v, a_v, u_v, xb, cb, sgb, gb_v,
    nsend, nrecv, sbuf,
    lsend, lrecv, lowb,
    pf, ps, rb, xsb, xrb,
    gp, csend, crecv, e_own, xsend, xrecv, zsend, zrecv,
    gms,
    loc_sem, gb_sem,
    zs, zr, x2s, x2r, c3s, c3r,
    cs, cr,
    n1s, n1r, n2s, n2r, l1s, l1r, l2s, l2r, gs, gr,
    pss, prs, pxs, pxr,
    bcs, bcr, bxs, bxr, bzs, bzr,
):
    col = lax.axis_index("col")
    row = lax.axis_index("row")
    z, xl, c = col // 4, (col // 2) % 2, col % 2
    y, xh = row // 2, row % 2
    cols = w_v.shape[1]
    width = w_v.shape[0]

    def at_col(zz, xx, cc):
        return {"col": (zz * 2 + xx) * 2 + cc, "row": row}

    def at_row(rr):
        return {"col": col, "row": rr}

    core_mate = at_col(z, xl, 1 - c)
    x_mate = at_col(z, 1 - xl, c)
    y_up = at_row(((y + 1) % NY) * 2 + xh)
    y_down = at_row(((y + NY - 1) % NY) * 2 + xh)
    far_mate = at_row(y * 2 + 1 - xh)

    def rcopy(src, dst, ssem, rsem, dev):
        return pltpu.make_async_remote_copy(
            src_ref=src, dst_ref=dst, send_sem=ssem, recv_sem=rsem,
            device_id=dev, device_id_type=MESH,
        )

    def got(dst, rsem):
        rcopy(dst, dst, rsem, rsem, core_mate).wait_recv()

    def sent(src, ssem):
        rcopy(src, src, ssem, ssem, core_mate).wait_send()

    def block_tenant(b):
        return ten[b * 128]

    loads = [
        pltpu.make_async_copy(x_in, xb.at[z, c, xl], loc_sem.at[0]),
        pltpu.make_async_copy(w_in, w_v, loc_sem.at[1]),
        pltpu.make_async_copy(a_in, a_v, loc_sem.at[2]),
        pltpu.make_async_copy(u_in, u_v, loc_sem.at[3]),
        pltpu.make_async_copy(c_in, cb.at[row], loc_sem.at[4]),
    ]
    for one in loads:
        one.start()

    barrier = pltpu.get_barrier_semaphore()
    for o in range(1, NZ):
        pl.semaphore_signal(barrier, inc=1, device_id=at_col((z + o) % NZ, xl, c), device_id_type=MESH)
    for o in range(1, NR):
        pl.semaphore_signal(barrier, inc=1, device_id=at_row((row + o) % NR), device_id_type=MESH)
    pl.semaphore_signal(barrier, inc=1, device_id=x_mate, device_id_type=MESH)
    pl.semaphore_signal(barrier, inc=1, device_id=core_mate, device_id_type=MESH)
    pl.semaphore_wait(barrier, (NZ - 1) + (NR - 1) + 2)

    def zcopy(o):
        return rcopy(x_in, xb.at[z, c, xl], zs.at[o], zr.at[z], at_col((z + o) % NZ, xl, c))

    for o in (1, 7, 2, 6, 3, 5, 4):
        zcopy(o).start()

    def cot_copy(i, src, b, dev):
        return rcopy(src, cb.at[b], cs.at[i], cr.at[b], dev)

    b_far = y * 2 + 1 - xh
    b_dn = ((y + NY - 1) % NY) * 2 + xh
    b_upfar = ((y + 1) % NY) * 2 + 1 - xh
    cot_sends = [
        cot_copy(0, c_in, row, far_mate),
        cot_copy(1, c_in, row, y_up),
        cot_copy(2, c_in, row, y_down),
        cot_copy(3, cb.at[b_far], b_far, y_up),
        cot_copy(4, cb.at[b_far], b_far, y_down),
        cot_copy(5, cb.at[b_dn], b_dn, y_up),
        cot_copy(6, cb.at[b_upfar], b_upfar, y_down),
    ]
    for one in cot_sends[:3]:
        one.start()

    for one in loads:
        one.wait()
    a_all = a_v[...].reshape(NR * 2 * 16, width)
    aat = mm_nt(a_all, a_all)
    same = lax.broadcasted_iota(jnp.int32, aat.shape, 0) // 16 == lax.broadcasted_iota(jnp.int32, aat.shape, 1) // 16
    gram = jnp.where(same, aat, 0.0)
    gram_hi = gram.astype(BF)
    gram_lo = (gram - gram_hi.astype(F32)).astype(BF)
    for n0, n1 in lane_tiles(cols):
        wt = w_v[:, n0:n1]
        ut = u_v[:, :, n0:n1].reshape(256, n1 - n0)
        val = 2.0 * mm(a_all, wt) + (mm(gram_hi, ut) + mm(gram_lo, ut))
        quad = jnp.sum((ut.astype(F32) * val).reshape(16, 16, n1 - n0), axis=1)
        wf = wt.astype(F32)
        wsq = jnp.sum(jnp.sum((wf * wf).reshape(width // 8, 8, n1 - n0), axis=0), axis=0, keepdims=True)
        nsq = quad + wsq
        for r in range(NR):
            nsend[r, :, n0:n1] = nsq[2 * r:2 * r + 2]
    nrecv[row] = nsend[row]

    def n1copy(o):
        r = (row + o) % NR
        return rcopy(nsend.at[r], nrecv.at[row], n1s.at[o], n1r.at[row], at_row(r))

    for o in range(1, NR):
        n1copy(o).start()

    def n2copy(o):
        r = (row + o) % NR
        return rcopy(sbuf.at[row], sbuf.at[row], n2s.at[o], n2r.at[row], at_row(r))

    def l1copy(r):
        return rcopy(lsend.at[r], lrecv.at[row], l1s.at[r], l1r.at[row], at_row(r))

    def l2copy(o):
        r = (row + o) % NR
        return rcopy(lowb.at[row], lowb.at[row], l2s.at[o], l2r.at[row], at_row(r))

    def z_of(k):
        return (z + NZ + jnp.where(k % 2 == 1, (k + 1) // 2, -(k // 2))) % NZ

    def b_of(q):
        dy = jnp.where(q >= 6, 2, jnp.where(q % 3 == 2, 3, q % 3))
        dx = jnp.where(q >= 6, q - 6, q // 3)
        return ((y + dy) % NY) * 2 + (xh + dx) % 2

    def x2copy(zz):
        return rcopy(xb.at[zz, c, xl], xb.at[zz, c, xl], x2s.at[zz], x2r.at[zz], x_mate)

    def c3copy(zz):
        return rcopy(xb.at[zz, c], xb.at[zz, c], c3s.at[zz], c3r.at[zz], core_mate)

    def pre_slot(dy, xx):
        return jnp.where(dy == 2, 4 + xx, jnp.where(dy == 1, xx, 2 + xx))

    def pre_copy(dy, xx):
        slot = pre_slot(dy, xx)
        up = (dy == 1) | ((dy == 2) & (xx == 0))
        yy = jnp.where(up, (y + 1) % NY, (y + NY - 1) % NY)
        return rcopy(ps.at[dy, xx], rb.at[slot], pss.at[slot], prs.at[slot], at_row(yy * 2 + xh))

    far_copy = rcopy(xsb, xrb, pxs, pxr, far_mate)

    def bccopy(b):
        return rcopy(csend.at[b], crecv.at[b], bcs.at[b], bcr.at[b], core_mate)

    def bxcopy(b):
        return rcopy(xsend.at[b], xrecv.at[b], bxs.at[b], bxr.at[b], x_mate)

    def bzcopy(b):
        return rcopy(zsend.at[b], zrecv.at[z], bzs.at[b], bzr.at[z], at_col(b, xl, c))

    def forward_block(zz):
        xs = jnp.concatenate([xb[zz, 0, 0], xb[zz, 1, 0], xb[zz, 0, 1], xb[zz, 1, 1]], axis=0)
        dy = (zz // 2 + NY - y) % NY
        xx = zz % 2
        for n0, n1 in lane_tiles(cols):
            part = mm(xs, w_v[:, n0:n1])
            pf[dy, xx, :, n0:n1] = part
            ps[dy, xx, :, n0:n1] = part.astype(BF)
        low = mm_nt(a_v[block_tenant(zz)], xs)
        lsend[zz] = low

        @pl.when((dy == 2) | ((dy == 1) & (xx == 1)) | ((dy == 3) & (xx == 0)))
        def _():
            pre_copy(dy, xx).start()

        @pl.when(zz != row)
        def _():
            l1copy(zz).start()

        @pl.when(zz == row)
        def _():
            lrecv[row] = low

    def token_scale(b):
        t = block_tenant(b)
        s = sbuf[...]
        number = lax.broadcasted_iota(jnp.int32, s.shape, 0) * 2 + lax.broadcasted_iota(jnp.int32, s.shape, 1)
        return jnp.sum(jnp.sum(jnp.where(number == t, s, 0.0), axis=0), axis=0, keepdims=True)

    def backward_block(b):
        t = block_tenant(b)
        sg = (cb[b].astype(F32) * token_scale(b)).astype(BF)
        sgb[b] = sg
        u = u_v[t]
        a = a_v[t]
        back = mm_nt(sg, jnp.concatenate([u, u], axis=0))
        hi = back.astype(BF).astype(F32)
        lane = lax.broadcasted_iota(jnp.int32, back.shape, 1)
        both = jnp.where(lane < 16, hi, back - hi).astype(BF)
        a2 = jnp.concatenate([a, a], axis=0)
        for n0, n1 in lane_tiles(width):
            part = mm_nt(sg, w_v[n0:n1, :]) + mm(both, a2[:, n0:n1])
            gp[b, :, :, :, n0:n1] = part.reshape(2, 2, 32, n1 - n0)
        csend[b] = gp[b, :, 1 - c].astype(BF)
        bccopy(b).start()

    def step(s, carry):
        @pl.when(s < NZ)
        def _():
            zz = z_of(s)

            @pl.when(s > 0)
            def _():
                got(xb.at[zz, c, xl], zr.at[zz])

            x2copy(zz).start()

        @pl.when((s >= 1) & (s < NZ + 1))
        def _():
            zz = z_of(s - 1)
            got(xb.at[zz, c, 1 - xl], x2r.at[zz])
            c3copy(zz).start()

        @pl.when(s == 2)
        def _():
            got(cb.at[b_far], cr.at[b_far])
            cot_sends[3].start()
            cot_sends[4].start()

        @pl.when(s == 4)
        def _():
            got(cb.at[b_dn], cr.at[b_dn])
            cot_sends[5].start()
            for o in range(1, NR):
                r = (row + o) % NR
                got(nrecv.at[r], n1r.at[r])
            total = jnp.sum(nrecv[...], axis=0)
            m = mag[...]
            number = lax.broadcasted_iota(jnp.int32, m.shape, 0)
            mine = jnp.concatenate(
                [jnp.sum(jnp.where(number == 2 * row + i, m, 0.0), axis=0, keepdims=True) for i in range(2)], axis=0
            )
            sbuf[row] = mine / jnp.sqrt(total + EPS)
            for o in range(1, NR):
                n2copy(o).start()

        @pl.when((s >= 2) & (s < NZ + 2))
        def _():
            zz = z_of(s - 2)
            got(xb.at[zz, 1 - c], c3r.at[zz])
            forward_block(zz)

        @pl.when(s == FIRST_BACK)
        def _():
            for o in range(1, NR):
                r = (row + o) % NR
                got(sbuf.at[r], n2r.at[r])
            got(cb.at[b_upfar], cr.at[b_upfar])
            cot_sends[6].start()

        @pl.when(s == NZ + 2)
        def _():
            got(rb.at[4], prs.at[4])
            ps[1, 0] = (pf[1, 0] + rb[4].astype(F32)).astype(BF)
            pre_copy(1, 0).start()
            got(rb.at[5], prs.at[5])
            ps[3, 1] = (pf[3, 1] + rb[5].astype(F32)).astype(BF)
            pre_copy(3, 1).start()

        @pl.when(s == NZ + 4)
        def _():
            for o in range(1, NR):
                r = (row + o) % NR
                got(lrecv.at[r], l1r.at[r])
            lowb[row] = jnp.sum(lrecv[...], axis=0).astype(BF)
            for o in range(1, NR):
                l2copy(o).start()

        @pl.when((s >= FIRST_BACK) & (s < FIRST_BACK + NR))
        def _():
            q = s - FIRST_BACK
            b = b_of(q)

            @pl.when((q == 1) | (q >= 5))
            def _():
                got(cb.at[b], cr.at[b])

            backward_block(b)

        @pl.when((s >= FIRST_BACK + 1) & (s < FIRST_BACK + 1 + NR))
        def _():
            b = b_of(s - FIRST_BACK - 1)
            got(crecv.at[b], bcr.at[b])
            xsend[b] = (gp[b, 1 - xl, c] + crecv[b, 1 - xl].astype(F32)).astype(BF)
            bxcopy(b).start()
            e_own[b] = gp[b, xl, c] + crecv[b, xl].astype(F32)

        @pl.when(s >= FIRST_BACK + 2)
        def _():
            b = b_of(s - FIRST_BACK - 2)
            got(xrecv.at[b], bxr.at[b])
            both = e_own[b] + xrecv[b].astype(F32)
            zsend[b] = both.astype(BF)

            @pl.when(b != z)
            def _():
                bzcopy(b).start()

            @pl.when(b == z)
            def _():
                e_own[b] = both

        return carry

    lax.fori_loop(0, STEPS, step, 0)

    for slot in range(4):
        got(rb.at[slot], prs.at[slot])
    xx = 1 - xh
    xsb[...] = (pf[0, xx] + rb[xx].astype(F32) + rb[2 + xx].astype(F32)).astype(BF)
    far_copy.start()

    for o in range(1, NR):
        r = (row + o) % NR
        got(lowb.at[r], l2r.at[r])
    pieces = []
    for b in range(NR):
        wide = jnp.concatenate([lowb[b].astype(F32)] * 16, axis=0)
        number = lax.broadcasted_iota(jnp.int32, wide.shape, 0) // 16
        pieces.append(jnp.where(number == block_tenant(b), wide, 0.0).astype(BF))
    low_wide = jnp.concatenate(pieces, axis=1)
    for n0, n1 in lane_tiles(cols):
        sg = sgb[:, :, n0:n1].reshape(NR * 128, n1 - n0)
        gb_v[:, :, n0:n1] = mm(low_wide, sg).reshape(16, 16, n1 - n0)
    gb_out = pltpu.make_async_copy(gb_v, gb_ref, gb_sem)
    gb_out.start()

    got(xrb, pxr)
    u_mine = u_v[block_tenant(row)]
    low_mine = lowb[row].astype(F32).T.astype(BF)
    scale_mine = token_scale(row)
    for n0, n1 in lane_tiles(cols):
        pre = pf[0, xh, :, n0:n1] + rb[xh, :, n0:n1].astype(F32) + rb[2 + xh, :, n0:n1].astype(F32)
        pre = pre + xrb[:, n0:n1].astype(F32) + mm(low_mine, u_mine[:, n0:n1])
        result = (pre * scale_mine[:, n0:n1]).astype(BF)
        out_ref[:, n0:n1] = result
        product = cb[row, :, n0:n1].astype(F32) * result.astype(F32)
        gms[row, :, n0:n1] = jnp.sum(product, axis=0, keepdims=True)

    def gcopy(o):
        r = (row + o) % NR
        return rcopy(gms.at[row], gms.at[row], gs.at[o], gr.at[row], at_row(r))

    for o in range(1, NR):
        gcopy(o).start()

    for o in range(1, NZ):
        zz = (z + o) % NZ
        got(zrecv.at[zz], bzr.at[zz])
    total = e_own[z]
    for o in range(1, NZ):
        total = total + zrecv[(z + o) % NZ].astype(F32)
    gi_ref[...] = total.astype(BF)

    for o in range(1, NR):
        r = (row + o) % NR
        got(gms.at[r], gr.at[r])
    m = mag[...]
    number = lax.broadcasted_iota(jnp.int32, m.shape, 0)
    acc = jnp.zeros_like(m)
    for b in range(NR):
        acc = acc + jnp.where(number == block_tenant(b), gms[b], 0.0)
    gm_ref[...] = acc / m

    gb_out.wait()
    for o in range(1, NZ):
        sent(x_in, zs.at[o])
        sent(nsend.at[0], n1s.at[o])
        sent(sbuf.at[0], n2s.at[o])
        sent(lowb.at[0], l2s.at[o])
        sent(gms.at[0], gs.at[o])
    for k in range(NZ):
        sent(xb.at[k, 0, 0], x2s.at[k])
        sent(xb.at[k, 0], c3s.at[k])
        sent(csend.at[k], bcs.at[k])
        sent(xsend.at[k], bxs.at[k])

        @pl.when(k != z)
        def _():
            sent(zsend.at[k], bzs.at[k])

        @pl.when(k != row)
        def _():
            sent(lsend.at[k], l1s.at[k])
    for i in range(7):
        sent(c_in, cs.at[i])
    for i in range(6):
        sent(rb.at[i], pss.at[i])
    sent(xsb, pxs)


def shards(inputs, weight, adapter_down_factors, adapter_up_factors, magnitude, cotangent, tenant):
    width, cols = weight.shape
    tokens, rows = inputs.shape[0], cotangent.shape[0]
    any_, vmem = pl.BlockSpec(memory_space=pl.ANY), pl.BlockSpec(memory_space=pltpu.VMEM)
    dma = pltpu.SemaphoreType.DMA
    V = pltpu.VMEM
    return pl.pallas_call(
        kernel,
        out_shape=(
            jax.ShapeDtypeStruct((rows, cols), BF),
            jax.ShapeDtypeStruct((tokens, width), BF),
            jax.ShapeDtypeStruct((16, 16, cols), F32),
            jax.ShapeDtypeStruct((16, cols), F32),
        ),
        in_specs=[pl.BlockSpec(memory_space=pltpu.SMEM), any_, any_, any_, any_, vmem, any_],
        out_specs=(vmem, vmem, any_, vmem),
        scratch_shapes=[
            V((width, cols), BF), V((16, 16, width), BF), V((16, 16, cols), BF),
            V((NZ, 2, 2, tokens, width), BF), V((NR, rows, cols), BF), V((NR, rows, cols), BF),
            V((16, 16, cols), F32),
            V((NR, 2, cols), F32), V((NR, 2, cols), F32), V((NR, 2, cols), F32),
            V((NR, 16, rows), F32), V((NR, 16, rows), F32), V((NR, 16, rows), BF),
            V((NY, 2, rows, cols), F32), V((NY, 2, rows, cols), BF), V((6, rows, cols), BF),
            V((rows, cols), BF), V((rows, cols), BF),
            V((NR, 2, 2, tokens, width), F32), V((NR, 2, tokens, width), BF), V((NR, 2, tokens, width), BF),
            V((NR, tokens, width), F32),
            V((NR, tokens, width), BF), V((NR, tokens, width), BF),
            V((NR, tokens, width), BF), V((NR, tokens, width), BF),
            V((NR, 1, cols), F32),
            dma((5,)), dma,
            dma((8,)), dma((8,)), dma((8,)), dma((8,)), dma((8,)), dma((8,)),
            dma((7,)), dma((8,)),
            dma((8,)), dma((8,)), dma((8,)), dma((8,)), dma((8,)), dma((8,)), dma((8,)), dma((8,)), dma((8,)), dma((8,)),
            dma((6,)), dma((6,)), dma, dma,
            dma((8,)), dma((8,)), dma((8,)), dma((8,)), dma((8,)), dma((8,)),
        ],
        compiler_params=pltpu.CompilerParams(
            collective_id=0, has_side_effects=True, vmem_limit_bytes=56 << 20
        ),
        cost_estimate=pl.CostEstimate(flops=6 * 10**9, bytes_accessed=8 * 10**6, transcendentals=10**5),
        name="adapter_step",
    )(tenant, inputs, weight, adapter_down_factors, adapter_up_factors, magnitude, cotangent)


def solution(mesh):
    return jax.shard_map(
        shards,
        mesh=mesh,
        in_specs=(
            P("col", "row"),
            P("row", "col"),
            P(None, None, "row"),
            P(None, None, "col"),
            P(None, "col"),
            P("row", "col"),
            P(),
        ),
        out_specs=(P("row", "col"), P("col", "row"), P(None, None, "col"), P(None, "col")),
        check_vma=False,
    )
```

```python
import functools

import jax
import jax.numpy as jnp
from jax import lax
from jax.experimental import pallas as pl
from jax.experimental.pallas import tpu as pltpu
from jax.sharding import PartitionSpec as P

EPS = 1e-06
MESH = pl.DeviceIdType.MESH
BF = jnp.bfloat16
F32 = jnp.float32

NZ, NY, NR = 8, 4, 8
AT_FAR, AT_DOWN, AT_UPFAR = 2, 2, 6
AT_NORM, AT_SCALE, AT_VIA, AT_LOW = 1, 5, 13, 13
FIRST_BACK, LAG_X, LAG_Z = 5, 2, 4
FAR_OFF = 5
STEPS = FIRST_BACK + NZ + LAG_Z


def mm(a, b):
    return jnp.dot(a, b, preferred_element_type=F32)


def mm_nt(a, b):
    return lax.dot_general(a, b, (((1,), (1,)), ((), ())), preferred_element_type=F32)


def lane_tiles(width):
    return [(n, min(n + 256, width)) for n in range(0, width, 256)]


def kernel(
    ten, x_in, w_in, a_in, u_in, mag, c_in,
    out_ref, gi_ref, gb_ref, gm_ref,
    w_v, a_v, u_v, xb, cb, sgb, gb_v,
    nsend, nrecv, sbuf,
    lsend, lrecv, lowb,
    pf, ps, rb, xsb, xrb, rd,
    gp, csend, crecv, e_own, xsend, xrecv, zsend, zrecv,
    gms,
    loc_sem, gb_sem,
    zs, zr, x2s, x2r, c3s, c3r,
    cs, cr,
    n1s, n1r, n2s, n2r, l1s, l1r, l2s, l2r, gs, gr,
    pss, prs, pxs, pxr, ds, dr,
    bcs, bcr, bxs, bxr, bzs, bzr,
):
    col = lax.axis_index("col")
    row = lax.axis_index("row")
    z, xl, c = col // 4, (col // 2) % 2, col % 2
    y, xh = row // 2, row % 2
    cols = w_v.shape[1]
    width = w_v.shape[0]

    def at_col(zz, xx, cc):
        return {"col": (zz * 2 + xx) * 2 + cc, "row": row}

    def at_row(rr):
        return {"col": col, "row": rr}

    core_mate = at_col(z, xl, 1 - c)
    x_mate = at_col(z, 1 - xl, c)
    y_up = at_row(((y + 1) % NY) * 2 + xh)
    y_down = at_row(((y + NY - 1) % NY) * 2 + xh)
    far_mate = at_row(y * 2 + 1 - xh)

    def rcopy(src, dst, ssem, rsem, dev):
        return pltpu.make_async_remote_copy(
            src_ref=src, dst_ref=dst, send_sem=ssem, recv_sem=rsem,
            device_id=dev, device_id_type=MESH,
        )

    def got(dst, rsem):
        rcopy(dst, dst, rsem, rsem, core_mate).wait_recv()

    def sent(src, ssem):
        rcopy(src, src, ssem, ssem, core_mate).wait_send()

    def block_tenant(b):
        return ten[b * 128]

    loads = [
        pltpu.make_async_copy(x_in, xb.at[z, c, xl], loc_sem.at[0]),
        pltpu.make_async_copy(w_in, w_v, loc_sem.at[1]),
        pltpu.make_async_copy(a_in, a_v, loc_sem.at[2]),
        pltpu.make_async_copy(u_in, u_v, loc_sem.at[3]),
        pltpu.make_async_copy(c_in, cb.at[row], loc_sem.at[4]),
    ]
    for one in loads:
        one.start()

    barrier = pltpu.get_barrier_semaphore()
    for o in range(1, NZ):
        pl.semaphore_signal(barrier, inc=1, device_id=at_col((z + o) % NZ, xl, c), device_id_type=MESH)
    for o in range(1, NR):
        pl.semaphore_signal(barrier, inc=1, device_id=at_row((row + o) % NR), device_id_type=MESH)
    pl.semaphore_signal(barrier, inc=1, device_id=x_mate, device_id_type=MESH)
    pl.semaphore_signal(barrier, inc=1, device_id=core_mate, device_id_type=MESH)
    pl.semaphore_wait(barrier, (NZ - 1) + (NR - 1) + 2)

    z_up, z_down = at_col((z + 1) % NZ, xl, c), at_col((z + NZ - 1) % NZ, xl, c)

    def ring_place(slab, h, way):
        if h < 4:
            return xb.at[slab, c, xl], zr.at[slab, 0]
        return xb.at[slab, c, xl, pl.ds(16 * way, 16)], zr.at[slab, way]

    def ring(way, h):
        slab = (z + NZ - h) % NZ if way == 0 else (z + h) % NZ
        place, arrived = ring_place(slab, h + 1, way)
        src = x_in if h == 0 else place
        return rcopy(src, place, zs.at[way, h], arrived, z_up if way == 0 else z_down)

    def ring_got(way, h):
        slab = (z + NZ - h) % NZ if way == 0 else (z + h) % NZ
        got(*ring_place(slab, h, way))

    def x2copy(zz, src=None):
        place = xb.at[zz, c, xl]
        return rcopy(place if src is None else src, place, x2s.at[zz], x2r.at[zz], x_mate)

    def x2_got(zz):
        got(xb.at[zz, c, 1 - xl], x2r.at[zz])

    ring(0, 0).start()
    ring(1, 0).start()
    x2copy(z, x_in).start()

    def c3copy(zz):
        return rcopy(xb.at[zz, c], xb.at[zz, c], c3s.at[zz], c3r.at[zz], core_mate)

    def cot_copy(i, src, b, dev):
        return rcopy(src, cb.at[b], cs.at[i], cr.at[b], dev)

    b_far = y * 2 + 1 - xh
    b_dn = ((y + NY - 1) % NY) * 2 + xh
    b_upfar = ((y + 1) % NY) * 2 + 1 - xh
    cot_sends = [
        cot_copy(0, c_in, row, far_mate),
        cot_copy(1, c_in, row, y_up),
        cot_copy(2, c_in, row, y_down),
        cot_copy(3, cb.at[b_far], b_far, y_up),
        cot_copy(4, cb.at[b_far], b_far, y_down),
        cot_copy(5, cb.at[b_dn], b_dn, y_up),
        cot_copy(6, cb.at[b_upfar], b_upfar, y_down),
    ]
    for one in cot_sends[:3]:
        one.start()

    for one in loads:
        one.wait()
    a_all = a_v[...].reshape(NR * 2 * 16, width)
    aat = mm_nt(a_all, a_all)
    same = lax.broadcasted_iota(jnp.int32, aat.shape, 0) // 16 == lax.broadcasted_iota(jnp.int32, aat.shape, 1) // 16
    gram = jnp.where(same, aat, 0.0)
    gram_hi = gram.astype(BF)
    gram_lo = (gram - gram_hi.astype(F32)).astype(BF)
    for n0, n1 in lane_tiles(cols):
        wt = w_v[:, n0:n1]
        ut = u_v[:, :, n0:n1].reshape(256, n1 - n0)
        val = 2.0 * mm(a_all, wt) + (mm(gram_hi, ut) + mm(gram_lo, ut))
        quad = jnp.sum((ut.astype(F32) * val).reshape(16, 16, n1 - n0), axis=1)
        wf = wt.astype(F32)
        wsq = jnp.sum(jnp.sum((wf * wf).reshape(width // 8, 8, n1 - n0), axis=0), axis=0, keepdims=True)
        nsq = quad + wsq
        for r in range(NR):
            nsend[r, :, n0:n1] = nsq[2 * r:2 * r + 2]
    nrecv[row] = nsend[row]

    def n1copy(o):
        r = (row + o) % NR
        return rcopy(nsend.at[r], nrecv.at[row], n1s.at[o], n1r.at[row], at_row(r))

    for o in range(1, NR):
        n1copy(o).start()

    def n2copy(o):
        r = (row + o) % NR
        return rcopy(sbuf.at[row], sbuf.at[row], n2s.at[o], n2r.at[row], at_row(r))

    def l1copy(r):
        return rcopy(lsend.at[r], lrecv.at[row], l1s.at[r], l1r.at[row], at_row(r))

    def l2copy(o):
        r = (row + o) % NR
        return rcopy(lowb.at[row], lowb.at[row], l2s.at[o], l2r.at[row], at_row(r))

    def z_of(k):
        return (z + NZ + jnp.where(k % 2 == 1, (k + 1) // 2, -(k // 2))) % NZ

    def b_of(q):
        dy = jnp.where(q >= 6, 2, jnp.where(q % 3 == 2, 3, q % 3))
        dx = jnp.where(q >= 6, q - 6, q // 3)
        return ((y + dy) % NY) * 2 + (xh + dx) % 2

    def pre_slot(dy, xx):
        return jnp.where(dy == 2, 4 + xx, jnp.where(dy == 1, xx, 2 + xx))

    def pre_copy(dy, xx):
        slot = pre_slot(dy, xx)
        up = (dy == 1) | ((dy == 2) & (xx == 0))
        yy = jnp.where(up, (y + 1) % NY, (y + NY - 1) % NY)
        return rcopy(ps.at[dy, xx], rb.at[slot], pss.at[slot], prs.at[slot], at_row(yy * 2 + xh))

    def late(zz):
        d = (zz - z + NZ) % NZ
        return (d >= FAR_OFF) & (d <= NZ - FAR_OFF)

    def direct_copy(zz):
        dy, xx = (zz // 2 + NY - y) % NY, zz % 2
        return rcopy(ps.at[dy, xx], rd.at[row], ds.at[zz], dr.at[row], at_row(zz))

    far_copy = rcopy(xsb, xrb, pxs, pxr, far_mate)

    def bccopy(b):
        return rcopy(csend.at[b], crecv.at[b], bcs.at[b], bcr.at[b], core_mate)

    def bxcopy(b):
        return rcopy(xsend.at[b], xrecv.at[b], bxs.at[b], bxr.at[b], x_mate)

    def bzcopy(b):
        return rcopy(zsend.at[b], zrecv.at[z], bzs.at[b], bzr.at[z], at_col(b, xl, c))

    z_add0, z_add1, z_far = ((y + 1) % NY) * 2, ((y + 3) % NY) * 2 + 1, y * 2 + 1 - xh
    z_two0, z_two1 = ((y + 2) % NY) * 2, ((y + 2) % NY) * 2 + 1
    z_dir1, z_dir3 = ((y + 1) % NY) * 2 + 1, ((y + 3) % NY) * 2

    def forward_block(zz):
        xs = jnp.concatenate([xb[zz, 0, 0], xb[zz, 1, 0], xb[zz, 0, 1], xb[zz, 1, 1]], axis=0)
        dy = (zz // 2 + NY - y) % NY
        xx = zz % 2
        for n0, n1 in lane_tiles(cols):
            part = mm(xs, w_v[:, n0:n1])
            pf[dy, xx, :, n0:n1] = part
            ps[dy, xx, :, n0:n1] = part.astype(BF)
        low = mm_nt(a_v[block_tenant(zz)], xs)
        lsend[zz] = low

        @pl.when(late(zz) & (zz != row))
        def _():
            direct_copy(zz).start()

        @pl.when((~late(zz)) & ((dy == 2) | ((dy == 1) & (xx == 1)) | ((dy == 3) & (xx == 0))))
        def _():
            pre_copy(dy, xx).start()

        @pl.when(zz != row)
        def _():
            l1copy(zz).start()

        @pl.when(zz == row)
        def _():
            lrecv[row] = low

    def token_scale(b):
        t = block_tenant(b)
        s = sbuf[...]
        number = lax.broadcasted_iota(jnp.int32, s.shape, 0) * 2 + lax.broadcasted_iota(jnp.int32, s.shape, 1)
        return jnp.sum(jnp.sum(jnp.where(number == t, s, 0.0), axis=0), axis=0, keepdims=True)

    def backward_block(b):
        t = block_tenant(b)
        sg = (cb[b].astype(F32) * token_scale(b)).astype(BF)
        sgb[b] = sg
        u = u_v[t]
        a = a_v[t]
        back = mm_nt(sg, jnp.concatenate([u, u], axis=0))
        hi = back.astype(BF).astype(F32)
        lane = lax.broadcasted_iota(jnp.int32, back.shape, 1)
        both = jnp.where(lane < 16, hi, back - hi).astype(BF)
        a2 = jnp.concatenate([a, a], axis=0)
        for n0, n1 in lane_tiles(width):
            part = mm_nt(sg, w_v[n0:n1, :]) + mm(both, a2[:, n0:n1])
            gp[b, :, :, :, n0:n1] = part.reshape(2, 2, 32, n1 - n0)
        csend[b] = gp[b, :, 1 - c].astype(BF)
        bccopy(b).start()

    def step(s, carry):
        for h, at in ((1, 0), (2, 2), (3, 4)):
            @pl.when(s == at)
            def _():
                for way in range(2):
                    ring_got(way, h)
                    ring(way, h).start()
                for zz in ((z + NZ - h) % NZ, (z + h) % NZ):
                    x2copy(zz).start()
                for zz in ((z + NZ - h + 1) % NZ, (z + h - 1) % NZ)[: 1 if h == 1 else 2]:
                    x2_got(zz)
                    c3copy(zz).start()

        @pl.when(s == 6)
        def _():
            ring_got(0, 4)
            ring_got(1, 4)
            x2copy((z + 4) % NZ).start()
            for zz in ((z + NZ - 3) % NZ, (z + 3) % NZ):
                x2_got(zz)
                c3copy(zz).start()

        @pl.when(s == 7)
        def _():
            x2_got((z + 4) % NZ)
            c3copy((z + 4) % NZ).start()

        @pl.when(s == AT_FAR)
        def _():
            got(cb.at[b_far], cr.at[b_far])
            cot_sends[3].start()
            cot_sends[4].start()

        @pl.when(s == AT_DOWN)
        def _():
            got(cb.at[b_dn], cr.at[b_dn])
            cot_sends[5].start()

        @pl.when(s == AT_NORM)
        def _():
            for o in range(1, NR):
                r = (row + o) % NR
                got(nrecv.at[r], n1r.at[r])
            total = jnp.sum(nrecv[...], axis=0)
            m = mag[...]
            number = lax.broadcasted_iota(jnp.int32, m.shape, 0)
            mine = jnp.concatenate(
                [jnp.sum(jnp.where(number == 2 * row + i, m, 0.0), axis=0, keepdims=True) for i in range(2)], axis=0
            )
            sbuf[row] = mine / jnp.sqrt(total + EPS)
            for o in range(1, NR):
                n2copy(o).start()

        @pl.when((s == 1) | ((s >= 3) & (s < NZ + 2)))
        def _():
            zz = z_of(jnp.where(s == 1, 0, s - 2))
            got(xb.at[zz, 1 - c], c3r.at[zz])
            forward_block(zz)

        @pl.when(s == AT_SCALE)
        def _():
            for o in range(1, NR):
                r = (row + o) % NR
                got(sbuf.at[r], n2r.at[r])

        @pl.when(s == AT_UPFAR)
        def _():
            got(cb.at[b_upfar], cr.at[b_upfar])
            cot_sends[6].start()

        @pl.when((s == AT_VIA) & ~late(z_add0))
        def _():
            got(rb.at[4], prs.at[4])
            ps[1, 0] = (pf[1, 0] + rb[4].astype(F32)).astype(BF)
            pre_copy(1, 0).start()

        @pl.when((s == AT_VIA) & ~late(z_add1))
        def _():
            got(rb.at[5], prs.at[5])
            ps[3, 1] = (pf[3, 1] + rb[5].astype(F32)).astype(BF)
            pre_copy(3, 1).start()

        @pl.when(s == AT_LOW)
        def _():
            for o in range(1, NR):
                r = (row + o) % NR
                got(lrecv.at[r], l1r.at[r])
            low = jnp.sum(lrecv[...], axis=0)
            lowb[row] = low.astype(BF)
            for o in range(1, NR):
                l2copy(o).start()
            low_mine = low.astype(BF).astype(F32).T.astype(BF)
            u_mine = u_v[block_tenant(row)]
            for n0, n1 in lane_tiles(cols):
                pf[0, xh, :, n0:n1] = pf[0, xh, :, n0:n1] + mm(low_mine, u_mine[:, n0:n1])

        @pl.when((s >= FIRST_BACK) & (s < FIRST_BACK + NR))
        def _():
            q = s - FIRST_BACK
            b = b_of(q)

            @pl.when((q == 1) | (q >= 5))
            def _():
                got(cb.at[b], cr.at[b])

            backward_block(b)

        @pl.when((s >= FIRST_BACK + LAG_X) & (s < FIRST_BACK + LAG_X + NR))
        def _():
            b = b_of(s - FIRST_BACK - LAG_X)
            got(crecv.at[b], bcr.at[b])
            xsend[b] = (gp[b, 1 - xl, c] + crecv[b, 1 - xl].astype(F32)).astype(BF)
            bxcopy(b).start()
            e_own[b] = gp[b, xl, c] + crecv[b, xl].astype(F32)

        @pl.when(s >= FIRST_BACK + LAG_Z)
        def _():
            b = b_of(s - FIRST_BACK - LAG_Z)
            got(xrecv.at[b], bxr.at[b])
            both = e_own[b] + xrecv[b].astype(F32)
            zsend[b] = both.astype(BF)

            @pl.when(b != z)
            def _():
                bzcopy(b).start()

            @pl.when(b == z)
            def _():
                e_own[b] = both

        return carry

    lax.fori_loop(0, STEPS, step, 0)

    def magnitude_part(b, carry):
        dy = (b // 2 + NY - y) % NY
        part = jnp.sum(cb[b].astype(F32) * pf[dy, b % 2], axis=0, keepdims=True)
        gms[row, b] = part * token_scale(b)
        return carry

    lax.fori_loop(0, NR, magnitude_part, 0)

    def gcopy(o):
        r = (row + o) % NR
        return rcopy(gms.at[row], gms.at[row], gs.at[o], gr.at[row], at_row(r))

    for o in range(1, NR):
        gcopy(o).start()

    @pl.when(~late(z_far))
    def _():
        xx = 1 - xh
        got(rb.at[xx], prs.at[xx])
        got(rb.at[2 + xx], prs.at[2 + xx])
        xsb[...] = (pf[0, xx] + rb[xx].astype(F32) + rb[2 + xx].astype(F32)).astype(BF)
        far_copy.start()

    for o in range(1, NR):
        r = (row + o) % NR
        got(lowb.at[r], l2r.at[r])
    pieces = []
    for b in range(NR):
        wide = jnp.concatenate([lowb[b].astype(F32)] * 16, axis=0)
        number = lax.broadcasted_iota(jnp.int32, wide.shape, 0) // 16
        pieces.append(jnp.where(number == block_tenant(b), wide, 0.0).astype(BF))
    low_wide = jnp.concatenate(pieces, axis=1)
    for n0, n1 in lane_tiles(cols):
        sg = sgb[:, :, n0:n1].reshape(NR * 128, n1 - n0)
        gb_v[:, :, n0:n1] = mm(low_wide, sg).reshape(16, 16, n1 - n0)
    gb_out = pltpu.make_async_copy(gb_v, gb_ref, gb_sem)
    gb_out.start()

    for o in range(1, NZ):
        zz = (z + o) % NZ
        got(zrecv.at[zz], bzr.at[zz])
    total = e_own[z]
    for o in range(1, NZ):
        total = total + zrecv[(z + o) % NZ].astype(F32)
    gi_ref[...] = total.astype(BF)

    scale_mine = token_scale(row)

    @pl.when(late(row))
    def _():
        for o in range(1, NR):
            r = (row + o) % NR
            got(rd.at[r], dr.at[r])
        for n0, n1 in lane_tiles(cols):
            pre = pf[0, xh, :, n0:n1]
            for o in range(1, NR):
                pre = pre + rd[(row + o) % NR, :, n0:n1].astype(F32)
            out_ref[:, n0:n1] = (pre * scale_mine[:, n0:n1]).astype(BF)

    @pl.when(~late(row))
    def _():
        got(rb.at[xh], prs.at[xh])
        got(rb.at[2 + xh], prs.at[2 + xh])
        got(xrb, pxr)
        for n0, n1 in lane_tiles(cols):
            pre = pf[0, xh, :, n0:n1] + rb[xh, :, n0:n1].astype(F32) + rb[2 + xh, :, n0:n1].astype(F32)
            pre = pre + xrb[:, n0:n1].astype(F32)
            out_ref[:, n0:n1] = (pre * scale_mine[:, n0:n1]).astype(BF)

    for o in range(1, NR):
        r = (row + o) % NR
        got(gms.at[r], gr.at[r])
    sums = jnp.sum(gms[...], axis=0)
    m = mag[...]
    number = lax.broadcasted_iota(jnp.int32, m.shape, 0)
    acc = jnp.zeros_like(m)
    for b in range(NR):
        acc = acc + jnp.where(number == block_tenant(b), sums[b], 0.0)
    gm_ref[...] = acc / m

    gb_out.wait()
    for o in range(1, NZ):
        sent(nsend.at[0], n1s.at[o])
        sent(sbuf.at[0], n2s.at[o])
        sent(lowb.at[0], l2s.at[o])
        sent(gms.at[0], gs.at[o])
    for k in range(NZ):
        sent(xb.at[k, 0, 0], x2s.at[k])
        sent(xb.at[k, 0], c3s.at[k])
        sent(csend.at[k], bcs.at[k])
        sent(xsend.at[k], bxs.at[k])

        @pl.when(k != z)
        def _():
            sent(zsend.at[k], bzs.at[k])

        @pl.when(k != row)
        def _():
            sent(lsend.at[k], l1s.at[k])
    for i in range(7):
        sent(c_in, cs.at[i])
    for slot, zz in enumerate((z_add0, z_dir1, z_dir3, z_add1, z_two0, z_two1)):
        @pl.when(~late(zz))
        def _():
            sent(rb.at[slot], pss.at[slot])

    for zz in range(NR):
        @pl.when(late(zz) & (zz != row))
        def _():
            sent(ps.at[0, 0], ds.at[zz])

    @pl.when(~late(z_far))
    def _():
        sent(xsb, pxs)

    for way in range(2):
        for h in range(4):
            sent(x_in if h < 3 else x_in.at[pl.ds(0, 16)], zs.at[way, h])


def hand_over(*refs):
    held, into, out = refs[8:12], refs[12], refs[13]
    ins = [pltpu.make_async_copy(refs[i], held[i], into.at[i]) for i in range(4)]
    outs = [pltpu.make_async_copy(held[i], refs[4 + i], out.at[i]) for i in range(4)]
    for one in ins:
        one.start()
    for i in range(4):
        ins[i].wait()
        outs[i].start()
    for one in outs:
        one.wait()


def shards(inputs, weight, adapter_down_factors, adapter_up_factors, magnitude, cotangent, tenant):
    width, cols = weight.shape
    tokens, rows = inputs.shape[0], cotangent.shape[0]
    any_, vmem = pl.BlockSpec(memory_space=pl.ANY), pl.BlockSpec(memory_space=pltpu.VMEM)
    dma = pltpu.SemaphoreType.DMA
    V = pltpu.VMEM
    parts = pl.pallas_call(
        kernel,
        out_shape=(
            jax.ShapeDtypeStruct((rows, cols), BF),
            jax.ShapeDtypeStruct((tokens, width), BF),
            jax.ShapeDtypeStruct((16, 16, cols), F32),
            jax.ShapeDtypeStruct((16, cols), F32),
        ),
        in_specs=[pl.BlockSpec(memory_space=pltpu.SMEM), any_, any_, any_, any_, vmem, any_],
        out_specs=(vmem, vmem, any_, vmem),
        scratch_shapes=[
            V((width, cols), BF), V((16, 16, width), BF), V((16, 16, cols), BF),
            V((NZ, 2, 2, tokens, width), BF), V((NR, rows, cols), BF), V((NR, rows, cols), BF),
            V((16, 16, cols), F32),
            V((NR, 2, cols), F32), V((NR, 2, cols), F32), V((NR, 2, cols), F32),
            V((NR, 16, rows), F32), V((NR, 16, rows), F32), V((NR, 16, rows), BF),
            V((NY, 2, rows, cols), F32), V((NY, 2, rows, cols), BF), V((6, rows, cols), BF),
            V((rows, cols), BF), V((rows, cols), BF), V((NR, rows, cols), BF),
            V((NR, 2, 2, tokens, width), F32), V((NR, 2, tokens, width), BF), V((NR, 2, tokens, width), BF),
            V((NR, tokens, width), F32),
            V((NR, tokens, width), BF), V((NR, tokens, width), BF),
            V((NR, tokens, width), BF), V((NR, tokens, width), BF),
            V((NR, NR, 1, cols), F32),
            dma((5,)), dma,
            dma((2, 4)), dma((8, 2)), dma((8,)), dma((8,)), dma((8,)), dma((8,)),
            dma((7,)), dma((8,)),
            dma((8,)), dma((8,)), dma((8,)), dma((8,)), dma((8,)), dma((8,)), dma((8,)), dma((8,)), dma((8,)), dma((8,)),
            dma((6,)), dma((6,)), dma, dma, dma((8,)), dma((8,)),
            dma((8,)), dma((8,)), dma((8,)), dma((8,)), dma((8,)), dma((8,)),
        ],
        compiler_params=pltpu.CompilerParams(
            collective_id=0, has_side_effects=True, vmem_limit_bytes=56 << 20
        ),
        cost_estimate=pl.CostEstimate(flops=6 * 10**9, bytes_accessed=8 * 10**6, transcendentals=10**5),
        name="adapter_step",
    )(tenant, inputs, weight, adapter_down_factors, adapter_up_factors, magnitude, cotangent)
    return pl.pallas_call(
        hand_over,
        out_shape=[jax.ShapeDtypeStruct(p.shape, p.dtype) for p in parts],
        in_specs=[any_] * 4,
        out_specs=[any_] * 4,
        scratch_shapes=[V(p.shape, p.dtype) for p in parts] + [dma((4,)), dma((4,))],
        name="hand_over",
    )(*parts)


def solution(mesh):
    return jax.shard_map(
        shards,
        mesh=mesh,
        in_specs=(
            P("col", "row"),
            P("row", "col"),
            P(None, None, "row"),
            P(None, None, "col"),
            P(None, "col"),
            P("row", "col"),
            P(),
        ),
        out_specs=(P("row", "col"), P("col", "row"), P(None, None, "col"), P(None, "col")),
        check_vma=False,
    )
```

```python
import functools

import jax
import jax.numpy as jnp
from jax import lax
from jax.experimental import pallas as pl
from jax.experimental.pallas import tpu as pltpu
from jax.sharding import PartitionSpec as P

EPS = 1e-06
MESH = pl.DeviceIdType.MESH
BF = jnp.bfloat16
F32 = jnp.float32

NZ, NY, NR = 8, 4, 8
AT_FAR, AT_DOWN, AT_UPFAR = 2, 2, 6
AT_NORM, AT_SCALE, AT_VIA, AT_LOW = 1, 4, 12, 14
FIRST_BACK, LAG_X, LAG_Z = 4, 2, 4
STEPS = FIRST_BACK + NZ + LAG_Z


def mm(a, b):
    return jnp.dot(a, b, preferred_element_type=F32)


def mm_nt(a, b):
    return lax.dot_general(a, b, (((1,), (1,)), ((), ())), preferred_element_type=F32)


def lane_tiles(width):
    return [(n, min(n + 256, width)) for n in range(0, width, 256)]


def kernel(
    ten, x_in, w_in, a_in, u_in, mag, c_in,
    out_ref, gi_ref, gb_ref, gm_ref,
    w_v, a_v, u_v, xb, cb, sgb, gb_v,
    nsend, nrecv, sbuf,
    lsend, lrecv, lowb,
    pf, ps, rb, xsb, xrb,
    gp, csend, crecv, e_own, xsend, xrecv, zsend, zrecv,
    gms,
    loc_sem, gb_sem,
    zs, zr, x2s, x2r, c3s, c3r,
    cs, cr,
    n1s, n1r, n2s, n2r, l1s, l1r, l2s, l2r, gs, gr,
    pss, prs, pxs, pxr,
    bcs, bcr, bxs, bxr, bzs, bzr,
):
    col = lax.axis_index("col")
    row = lax.axis_index("row")
    z, xl, c = col // 4, (col // 2) % 2, col % 2
    y, xh = row // 2, row % 2
    cols = w_v.shape[1]
    width = w_v.shape[0]

    def at_col(zz, xx, cc):
        return {"col": (zz * 2 + xx) * 2 + cc, "row": row}

    def at_row(rr):
        return {"col": col, "row": rr}

    core_mate = at_col(z, xl, 1 - c)
    x_mate = at_col(z, 1 - xl, c)
    y_up = at_row(((y + 1) % NY) * 2 + xh)
    y_down = at_row(((y + NY - 1) % NY) * 2 + xh)
    far_mate = at_row(y * 2 + 1 - xh)

    def rcopy(src, dst, ssem, rsem, dev):
        return pltpu.make_async_remote_copy(
            src_ref=src, dst_ref=dst, send_sem=ssem, recv_sem=rsem,
            device_id=dev, device_id_type=MESH,
        )

    def got(dst, rsem):
        rcopy(dst, dst, rsem, rsem, core_mate).wait_recv()

    def sent(src, ssem):
        rcopy(src, src, ssem, ssem, core_mate).wait_send()

    def block_tenant(b):
        return ten[b * 128]

    loads = [
        pltpu.make_async_copy(x_in, xb.at[z, c, xl], loc_sem.at[0]),
        pltpu.make_async_copy(w_in, w_v, loc_sem.at[1]),
        pltpu.make_async_copy(a_in, a_v, loc_sem.at[2]),
        pltpu.make_async_copy(u_in, u_v, loc_sem.at[3]),
        pltpu.make_async_copy(c_in, cb.at[row], loc_sem.at[4]),
    ]
    for one in loads:
        one.start()

    barrier = pltpu.get_barrier_semaphore()
    for o in range(1, NZ):
        pl.semaphore_signal(barrier, inc=1, device_id=at_col((z + o) % NZ, xl, c), device_id_type=MESH)
    for o in range(1, NR):
        pl.semaphore_signal(barrier, inc=1, device_id=at_row((row + o) % NR), device_id_type=MESH)
    pl.semaphore_signal(barrier, inc=1, device_id=x_mate, device_id_type=MESH)
    pl.semaphore_signal(barrier, inc=1, device_id=core_mate, device_id_type=MESH)
    pl.semaphore_wait(barrier, (NZ - 1) + (NR - 1) + 2)

    z_up, z_down = at_col((z + 1) % NZ, xl, c), at_col((z + NZ - 1) % NZ, xl, c)

    def ring_place(slab, h, way):
        if h < 4:
            return xb.at[slab, c, xl], zr.at[slab, 0]
        return xb.at[slab, c, xl, pl.ds(16 * way, 16)], zr.at[slab, way]

    def ring(way, h):
        slab = (z + NZ - h) % NZ if way == 0 else (z + h) % NZ
        place, arrived = ring_place(slab, h + 1, way)
        src = x_in if h == 0 else place
        return rcopy(src, place, zs.at[way, h], arrived, z_up if way == 0 else z_down)

    def ring_got(way, h):
        slab = (z + NZ - h) % NZ if way == 0 else (z + h) % NZ
        got(*ring_place(slab, h, way))

    def x2copy(zz, src=None):
        place = xb.at[zz, c, xl]
        return rcopy(place if src is None else src, place, x2s.at[zz], x2r.at[zz], x_mate)

    def x2_got(zz):
        got(xb.at[zz, c, 1 - xl], x2r.at[zz])

    ring(0, 0).start()
    ring(1, 0).start()
    x2copy(z, x_in).start()

    def c3copy(zz):
        return rcopy(xb.at[zz, c], xb.at[zz, c], c3s.at[zz], c3r.at[zz], core_mate)

    def cot_copy(i, src, b, dev):
        return rcopy(src, cb.at[b], cs.at[i], cr.at[b], dev)

    b_far = y * 2 + 1 - xh
    b_dn = ((y + NY - 1) % NY) * 2 + xh
    b_upfar = ((y + 1) % NY) * 2 + 1 - xh
    cot_sends = [
        cot_copy(0, c_in, row, far_mate),
        cot_copy(1, c_in, row, y_up),
        cot_copy(2, c_in, row, y_down),
        cot_copy(3, cb.at[b_far], b_far, y_up),
        cot_copy(4, cb.at[b_far], b_far, y_down),
        cot_copy(5, cb.at[b_dn], b_dn, y_up),
        cot_copy(6, cb.at[b_upfar], b_upfar, y_down),
    ]
    for one in cot_sends[:3]:
        one.start()

    for one in loads:
        one.wait()
    a_all = a_v[...].reshape(NR * 2 * 16, width)
    aat = mm_nt(a_all, a_all)
    same = lax.broadcasted_iota(jnp.int32, aat.shape, 0) // 16 == lax.broadcasted_iota(jnp.int32, aat.shape, 1) // 16
    gram = jnp.where(same, aat, 0.0)
    gram_hi = gram.astype(BF)
    gram_lo = (gram - gram_hi.astype(F32)).astype(BF)
    for n0, n1 in lane_tiles(cols):
        wt = w_v[:, n0:n1]
        ut = u_v[:, :, n0:n1].reshape(256, n1 - n0)
        val = 2.0 * mm(a_all, wt) + (mm(gram_hi, ut) + mm(gram_lo, ut))
        quad = jnp.sum((ut.astype(F32) * val).reshape(16, 16, n1 - n0), axis=1)
        wf = wt.astype(F32)
        wsq = jnp.sum(jnp.sum((wf * wf).reshape(width // 8, 8, n1 - n0), axis=0), axis=0, keepdims=True)
        nsq = quad + wsq
        for r in range(NR):
            nsend[r, :, n0:n1] = nsq[2 * r:2 * r + 2]
    nrecv[row] = nsend[row]

    def n1copy(o):
        r = (row + o) % NR
        return rcopy(nsend.at[r], nrecv.at[row], n1s.at[o], n1r.at[row], at_row(r))

    for o in range(1, NR):
        n1copy(o).start()

    def n2copy(o):
        r = (row + o) % NR
        return rcopy(sbuf.at[row], sbuf.at[row], n2s.at[o], n2r.at[row], at_row(r))

    def l1copy(r):
        return rcopy(lsend.at[r], lrecv.at[row], l1s.at[r], l1r.at[row], at_row(r))

    def l2copy(o):
        r = (row + o) % NR
        return rcopy(lowb.at[row], lowb.at[row], l2s.at[o], l2r.at[row], at_row(r))

    def z_of(k):
        return (z + NZ + jnp.where(k % 2 == 1, (k + 1) // 2, -(k // 2))) % NZ

    def b_of(q):
        dy = jnp.where(q >= 6, 2, jnp.where(q % 3 == 2, 3, q % 3))
        dx = jnp.where(q >= 6, q - 6, q // 3)
        return ((y + dy) % NY) * 2 + (xh + dx) % 2

    def pre_slot(dy, xx):
        return jnp.where(dy == 2, 4 + xx, jnp.where(dy == 1, xx, 2 + xx))

    def pre_copy(dy, xx, half):
        slot = pre_slot(dy, xx)
        up = (dy == 1) | ((dy == 2) & (xx == 0))
        yy = jnp.where(up, (y + 1) % NY, (y + NY - 1) % NY)
        part = pl.ds(64 * half, 64)
        return rcopy(
            ps.at[dy, xx, part], rb.at[slot, part], pss.at[slot, half], prs.at[slot, half], at_row(yy * 2 + xh)
        )

    def pre_got(slot, half):
        got(rb.at[slot, pl.ds(64 * half, 64)], prs.at[slot, half])

    def far_copy(half):
        part = pl.ds(64 * half, 64)
        return rcopy(xsb.at[part], xrb.at[part], pxs.at[half], pxr.at[half], far_mate)

    def bccopy(b):
        return rcopy(csend.at[b], crecv.at[b], bcs.at[b], bcr.at[b], core_mate)

    def bxcopy(b):
        return rcopy(xsend.at[b], xrecv.at[b], bxs.at[b], bxr.at[b], x_mate)

    def bzcopy(b):
        return rcopy(zsend.at[b], zrecv.at[z], bzs.at[b], bzr.at[z], at_col(b, xl, c))

    def forward_block(zz):
        xs = jnp.concatenate([xb[zz, 0, 0], xb[zz, 1, 0], xb[zz, 0, 1], xb[zz, 1, 1]], axis=0)
        dy = (zz // 2 + NY - y) % NY
        xx = zz % 2
        for n0, n1 in lane_tiles(cols):
            part = mm(xs, w_v[:, n0:n1])
            pf[dy, xx, :, n0:n1] = part
            ps[dy, xx, :, n0:n1] = part.astype(BF)
        low = mm_nt(a_v[block_tenant(zz)], xs)
        lsend[zz] = low

        @pl.when((dy == 2) | ((dy == 1) & (xx == 1)) | ((dy == 3) & (xx == 0)))
        def _():
            for half in range(2):
                pre_copy(dy, xx, half).start()

        @pl.when(zz != row)
        def _():
            l1copy(zz).start()

        @pl.when(zz == row)
        def _():
            lrecv[row] = low

    def token_scale(b):
        t = block_tenant(b)
        s = sbuf[...]
        number = lax.broadcasted_iota(jnp.int32, s.shape, 0) * 2 + lax.broadcasted_iota(jnp.int32, s.shape, 1)
        return jnp.sum(jnp.sum(jnp.where(number == t, s, 0.0), axis=0), axis=0, keepdims=True)

    def backward_block(b):
        t = block_tenant(b)
        sg = (cb[b].astype(F32) * token_scale(b)).astype(BF)
        sgb[b] = sg
        u = u_v[t]
        a = a_v[t]
        back = mm_nt(sg, jnp.concatenate([u, u], axis=0))
        hi = back.astype(BF).astype(F32)
        lane = lax.broadcasted_iota(jnp.int32, back.shape, 1)
        both = jnp.where(lane < 16, hi, back - hi).astype(BF)
        a2 = jnp.concatenate([a, a], axis=0)
        for n0, n1 in lane_tiles(width):
            part = mm_nt(sg, w_v[n0:n1, :]) + mm(both, a2[:, n0:n1])
            gp[b, :, :, :, n0:n1] = part.reshape(2, 2, 32, n1 - n0)
        csend[b] = gp[b, :, 1 - c].astype(BF)
        bccopy(b).start()

    def step(s, carry):
        for h, at in ((1, 0), (2, 2), (3, 4)):
            @pl.when(s == at)
            def _():
                for way in range(2):
                    ring_got(way, h)
                    ring(way, h).start()
                for zz in ((z + NZ - h) % NZ, (z + h) % NZ):
                    x2copy(zz).start()
                for zz in ((z + NZ - h + 1) % NZ, (z + h - 1) % NZ)[: 1 if h == 1 else 2]:
                    x2_got(zz)
                    c3copy(zz).start()

        @pl.when(s == 6)
        def _():
            ring_got(0, 4)
            ring_got(1, 4)
            x2copy((z + 4) % NZ).start()
            for zz in ((z + NZ - 3) % NZ, (z + 3) % NZ):
                x2_got(zz)
                c3copy(zz).start()

        @pl.when(s == 7)
        def _():
            x2_got((z + 4) % NZ)
            c3copy((z + 4) % NZ).start()

        @pl.when(s == AT_FAR)
        def _():
            got(cb.at[b_far], cr.at[b_far])
            cot_sends[3].start()
            cot_sends[4].start()

        @pl.when(s == AT_DOWN)
        def _():
            got(cb.at[b_dn], cr.at[b_dn])
            cot_sends[5].start()

        @pl.when(s == AT_NORM)
        def _():
            for o in range(1, NR):
                r = (row + o) % NR
                got(nrecv.at[r], n1r.at[r])
            total = jnp.sum(nrecv[...], axis=0)
            m = mag[...]
            number = lax.broadcasted_iota(jnp.int32, m.shape, 0)
            mine = jnp.concatenate(
                [jnp.sum(jnp.where(number == 2 * row + i, m, 0.0), axis=0, keepdims=True) for i in range(2)], axis=0
            )
            sbuf[row] = mine / jnp.sqrt(total + EPS)
            for o in range(1, NR):
                n2copy(o).start()

        @pl.when((s == 1) | ((s >= 3) & (s < NZ + 2)))
        def _():
            zz = z_of(jnp.where(s == 1, 0, s - 2))
            got(xb.at[zz, 1 - c], c3r.at[zz])
            forward_block(zz)

        @pl.when(s == AT_SCALE)
        def _():
            for o in range(1, NR):
                r = (row + o) % NR
                got(sbuf.at[r], n2r.at[r])

        @pl.when(s == AT_UPFAR)
        def _():
            got(cb.at[b_upfar], cr.at[b_upfar])
            cot_sends[6].start()

        @pl.when(s == AT_LOW)
        def _():
            for o in range(1, NR):
                r = (row + o) % NR
                got(lrecv.at[r], l1r.at[r])
            low = jnp.sum(lrecv[...], axis=0)
            lowb[row] = low.astype(BF)
            for o in range(1, NR):
                l2copy(o).start()
            low_mine = low.astype(BF).astype(F32).T.astype(BF)
            u_mine = u_v[block_tenant(row)]
            for n0, n1 in lane_tiles(cols):
                pf[0, xh, :, n0:n1] = pf[0, xh, :, n0:n1] + mm(low_mine, u_mine[:, n0:n1])

        @pl.when((s >= FIRST_BACK) & (s < FIRST_BACK + NR))
        def _():
            q = s - FIRST_BACK
            b = b_of(q)

            @pl.when((q == 1) | (q >= 5))
            def _():
                got(cb.at[b], cr.at[b])

            backward_block(b)

        @pl.when((s >= FIRST_BACK + LAG_X) & (s < FIRST_BACK + LAG_X + NR))
        def _():
            b = b_of(s - FIRST_BACK - LAG_X)
            got(crecv.at[b], bcr.at[b])
            xsend[b] = (gp[b, 1 - xl, c] + crecv[b, 1 - xl].astype(F32)).astype(BF)
            bxcopy(b).start()
            e_own[b] = gp[b, xl, c] + crecv[b, xl].astype(F32)

        @pl.when(s >= FIRST_BACK + LAG_Z)
        def _():
            b = b_of(s - FIRST_BACK - LAG_Z)
            got(xrecv.at[b], bxr.at[b])
            both = e_own[b] + xrecv[b].astype(F32)
            zsend[b] = both.astype(BF)

            @pl.when(b != z)
            def _():
                bzcopy(b).start()

            @pl.when(b == z)
            def _():
                e_own[b] = both

        @pl.when(s == AT_VIA)
        def _():
            for half in range(2):
                rows = pl.ds(64 * half, 64)
                for slot, dy, xx in ((4, 1, 0), (5, 3, 1)):
                    pre_got(slot, half)
                    ps[dy, xx, rows] = (pf[dy, xx, rows] + rb[slot, rows].astype(F32)).astype(BF)
                    pre_copy(dy, xx, half).start()

        return carry

    lax.fori_loop(0, STEPS, step, 0)

    def magnitude_part(b, carry):
        dy = (b // 2 + NY - y) % NY
        part = jnp.sum(cb[b].astype(F32) * pf[dy, b % 2], axis=0, keepdims=True)
        gms[row, b] = part * token_scale(b)
        return carry

    lax.fori_loop(0, NR, magnitude_part, 0)

    def gcopy(o):
        r = (row + o) % NR
        return rcopy(gms.at[row], gms.at[row], gs.at[o], gr.at[row], at_row(r))

    for o in range(1, NR):
        gcopy(o).start()

    xx = 1 - xh
    for half in range(2):
        rows = pl.ds(64 * half, 64)
        pre_got(xx, half)
        pre_got(2 + xx, half)
        xsb[rows] = (pf[0, xx, rows] + rb[xx, rows].astype(F32) + rb[2 + xx, rows].astype(F32)).astype(BF)
        far_copy(half).start()

    for o in range(1, NR):
        r = (row + o) % NR
        got(lowb.at[r], l2r.at[r])
    pieces = []
    for b in range(NR):
        wide = jnp.concatenate([lowb[b].astype(F32)] * 16, axis=0)
        number = lax.broadcasted_iota(jnp.int32, wide.shape, 0) // 16
        pieces.append(jnp.where(number == block_tenant(b), wide, 0.0).astype(BF))
    low_wide = jnp.concatenate(pieces, axis=1)
    for n0, n1 in lane_tiles(cols):
        sg = sgb[:, :, n0:n1].reshape(NR * 128, n1 - n0)
        gb_v[:, :, n0:n1] = mm(low_wide, sg).reshape(16, 16, n1 - n0)
    gb_out = pltpu.make_async_copy(gb_v, gb_ref, gb_sem)
    gb_out.start()

    for o in range(1, NZ):
        zz = (z + o) % NZ
        got(zrecv.at[zz], bzr.at[zz])
    total = e_own[z]
    for o in range(1, NZ):
        total = total + zrecv[(z + o) % NZ].astype(F32)
    gi_ref[...] = total.astype(BF)

    scale_mine = token_scale(row)

    for half in range(2):
        rows = pl.ds(64 * half, 64)
        pre_got(xh, half)
        pre_got(2 + xh, half)
        got(xrb.at[rows], pxr.at[half])
        for n0, n1 in lane_tiles(cols):
            pre = pf[0, xh, rows, n0:n1] + rb[xh, rows, n0:n1].astype(F32) + rb[2 + xh, rows, n0:n1].astype(F32)
            pre = pre + xrb[rows, n0:n1].astype(F32)
            out_ref[rows, n0:n1] = (pre * scale_mine[:, n0:n1]).astype(BF)

    for o in range(1, NR):
        r = (row + o) % NR
        got(gms.at[r], gr.at[r])
    sums = jnp.sum(gms[...], axis=0)
    m = mag[...]
    number = lax.broadcasted_iota(jnp.int32, m.shape, 0)
    acc = jnp.zeros_like(m)
    for b in range(NR):
        acc = acc + jnp.where(number == block_tenant(b), sums[b], 0.0)
    gm_ref[...] = acc / m

    gb_out.wait()
    for o in range(1, NZ):
        sent(nsend.at[0], n1s.at[o])
        sent(sbuf.at[0], n2s.at[o])
        sent(lowb.at[0], l2s.at[o])
        sent(gms.at[0], gs.at[o])
    for k in range(NZ):
        sent(xb.at[k, 0, 0], x2s.at[k])
        sent(xb.at[k, 0], c3s.at[k])
        sent(csend.at[k], bcs.at[k])
        sent(xsend.at[k], bxs.at[k])

        @pl.when(k != z)
        def _():
            sent(zsend.at[k], bzs.at[k])

        @pl.when(k != row)
        def _():
            sent(lsend.at[k], l1s.at[k])
    for i in range(7):
        sent(c_in, cs.at[i])
    for half in range(2):
        rows = pl.ds(64 * half, 64)
        for slot in range(6):
            sent(rb.at[slot, rows], pss.at[slot, half])
        sent(xsb.at[rows], pxs.at[half])
    for way in range(2):
        for h in range(4):
            sent(x_in if h < 3 else x_in.at[pl.ds(0, 16)], zs.at[way, h])


def hand_over(*refs):
    held, into, out = refs[8:12], refs[12], refs[13]
    ins = [pltpu.make_async_copy(refs[i], held[i], into.at[i]) for i in range(4)]
    outs = [pltpu.make_async_copy(held[i], refs[4 + i], out.at[i]) for i in range(4)]
    for one in ins:
        one.start()
    for i in range(4):
        ins[i].wait()
        outs[i].start()
    for one in outs:
        one.wait()


def shards(inputs, weight, adapter_down_factors, adapter_up_factors, magnitude, cotangent, tenant):
    width, cols = weight.shape
    tokens, rows = inputs.shape[0], cotangent.shape[0]
    any_, vmem = pl.BlockSpec(memory_space=pl.ANY), pl.BlockSpec(memory_space=pltpu.VMEM)
    dma = pltpu.SemaphoreType.DMA
    V = pltpu.VMEM
    parts = pl.pallas_call(
        kernel,
        out_shape=(
            jax.ShapeDtypeStruct((rows, cols), BF),
            jax.ShapeDtypeStruct((tokens, width), BF),
            jax.ShapeDtypeStruct((16, 16, cols), F32),
            jax.ShapeDtypeStruct((16, cols), F32),
        ),
        in_specs=[pl.BlockSpec(memory_space=pltpu.SMEM), any_, any_, any_, any_, vmem, any_],
        out_specs=(vmem, vmem, any_, vmem),
        scratch_shapes=[
            V((width, cols), BF), V((16, 16, width), BF), V((16, 16, cols), BF),
            V((NZ, 2, 2, tokens, width), BF), V((NR, rows, cols), BF), V((NR, rows, cols), BF),
            V((16, 16, cols), F32),
            V((NR, 2, cols), F32), V((NR, 2, cols), F32), V((NR, 2, cols), F32),
            V((NR, 16, rows), F32), V((NR, 16, rows), F32), V((NR, 16, rows), BF),
            V((NY, 2, rows, cols), F32), V((NY, 2, rows, cols), BF), V((6, rows, cols), BF),
            V((rows, cols), BF), V((rows, cols), BF),
            V((NR, 2, 2, tokens, width), F32), V((NR, 2, tokens, width), BF), V((NR, 2, tokens, width), BF),
            V((NR, tokens, width), F32),
            V((NR, tokens, width), BF), V((NR, tokens, width), BF),
            V((NR, tokens, width), BF), V((NR, tokens, width), BF),
            V((NR, NR, 1, cols), F32),
            dma((5,)), dma,
            dma((2, 4)), dma((8, 2)), dma((8,)), dma((8,)), dma((8,)), dma((8,)),
            dma((7,)), dma((8,)),
            dma((8,)), dma((8,)), dma((8,)), dma((8,)), dma((8,)), dma((8,)), dma((8,)), dma((8,)), dma((8,)), dma((8,)),
            dma((6, 2)), dma((6, 2)), dma((2,)), dma((2,)),
            dma((8,)), dma((8,)), dma((8,)), dma((8,)), dma((8,)), dma((8,)),
        ],
        compiler_params=pltpu.CompilerParams(
            collective_id=0, has_side_effects=True, vmem_limit_bytes=56 << 20
        ),
        cost_estimate=pl.CostEstimate(flops=6 * 10**9, bytes_accessed=8 * 10**6, transcendentals=10**5),
        name="adapter_step",
    )(tenant, inputs, weight, adapter_down_factors, adapter_up_factors, magnitude, cotangent)
    return pl.pallas_call(
        hand_over,
        out_shape=[jax.ShapeDtypeStruct(p.shape, p.dtype) for p in parts],
        in_specs=[any_] * 4,
        out_specs=[any_] * 4,
        scratch_shapes=[V(p.shape, p.dtype) for p in parts] + [dma((4,)), dma((4,))],
        name="hand_over",
    )(*parts)


def solution(mesh):
    return jax.shard_map(
        shards,
        mesh=mesh,
        in_specs=(
            P("col", "row"),
            P("row", "col"),
            P(None, None, "row"),
            P(None, None, "col"),
            P(None, "col"),
            P("row", "col"),
            P(),
        ),
        out_specs=(P("row", "col"), P("col", "row"), P(None, None, "col"), P(None, "col")),
        check_vma=False,
    )
```

```python
import functools

import jax
import jax.numpy as jnp
from jax import lax
from jax.experimental import pallas as pl
from jax.experimental.pallas import tpu as pltpu
from jax.sharding import PartitionSpec as P

EPS = 1e-06
MESH = pl.DeviceIdType.MESH
BF = jnp.bfloat16
F32 = jnp.float32

NZ, NY, NR = 8, 4, 8
AT_FAR, AT_DOWN, AT_UPFAR = 2, 2, 6
AT_NORM, AT_SCALE, AT_VIA, AT_LOW = 1, 4, 12, 14
FIRST_BACK, LAG_X, LAG_Z = 4, 2, 4
STEPS = FIRST_BACK + NZ + LAG_Z


def mm(a, b):
    return jnp.dot(a, b, preferred_element_type=F32)


def mm_nt(a, b):
    return lax.dot_general(a, b, (((1,), (1,)), ((), ())), preferred_element_type=F32)


def lane_tiles(width):
    return [(n, min(n + 256, width)) for n in range(0, width, 256)]


def kernel(
    ten, x_in, w_in, a_in, u_in, mag, c_in,
    out_ref, gi_ref, gb_ref, gm_ref,
    w_v, a_v, u_v, xb, cb, sgb, gb_v,
    nsend, nrecv, sbuf,
    lsend, lrecv, lowb,
    pf, ps, rb, xsb, xrb,
    gp, csend, crecv, e_own, xsend, xrecv, zsend, zrecv,
    gms,
    loc_sem, gb_sem,
    zs, zr, x2s, x2r, c3s, c3r,
    cs, cr,
    n1s, n1r, n2s, n2r, l1s, l1r, l2s, l2r, gs, gr,
    pss, prs, pxs, pxr,
    bcs, bcr, bxs, bxr, bzs, bzr,
):
    col = lax.axis_index("col")
    row = lax.axis_index("row")
    z, xl, c = col // 4, (col // 2) % 2, col % 2
    y, xh = row // 2, row % 2
    cols = w_v.shape[1]
    width = w_v.shape[0]

    def at_col(zz, xx, cc):
        return {"col": (zz * 2 + xx) * 2 + cc, "row": row}

    def at_row(rr):
        return {"col": col, "row": rr}

    core_mate = at_col(z, xl, 1 - c)
    x_mate = at_col(z, 1 - xl, c)
    y_up = at_row(((y + 1) % NY) * 2 + xh)
    y_down = at_row(((y + NY - 1) % NY) * 2 + xh)
    far_mate = at_row(y * 2 + 1 - xh)

    def rcopy(src, dst, ssem, rsem, dev):
        return pltpu.make_async_remote_copy(
            src_ref=src, dst_ref=dst, send_sem=ssem, recv_sem=rsem,
            device_id=dev, device_id_type=MESH,
        )

    def got(dst, rsem):
        rcopy(dst, dst, rsem, rsem, core_mate).wait_recv()

    def sent(src, ssem):
        rcopy(src, src, ssem, ssem, core_mate).wait_send()

    def block_tenant(b):
        return ten[b * 128]

    loads = [
        pltpu.make_async_copy(x_in, xb.at[z, c, xl], loc_sem.at[0]),
        pltpu.make_async_copy(w_in, w_v, loc_sem.at[1]),
        pltpu.make_async_copy(a_in, a_v, loc_sem.at[2]),
        pltpu.make_async_copy(u_in, u_v, loc_sem.at[3]),
        pltpu.make_async_copy(c_in, cb.at[row], loc_sem.at[4]),
    ]
    for one in loads:
        one.start()

    barrier = pltpu.get_barrier_semaphore()
    for o in range(1, NZ):
        pl.semaphore_signal(barrier, inc=1, device_id=at_col((z + o) % NZ, xl, c), device_id_type=MESH)
    for o in range(1, NR):
        pl.semaphore_signal(barrier, inc=1, device_id=at_row((row + o) % NR), device_id_type=MESH)
    pl.semaphore_signal(barrier, inc=1, device_id=x_mate, device_id_type=MESH)
    pl.semaphore_signal(barrier, inc=1, device_id=core_mate, device_id_type=MESH)
    pl.semaphore_wait(barrier, (NZ - 1) + (NR - 1) + 2)

    z_up, z_down = at_col((z + 1) % NZ, xl, c), at_col((z + NZ - 1) % NZ, xl, c)

    def ring_place(slab, h, way):
        if h < 4:
            return xb.at[slab, c, xl], zr.at[slab, 0]
        return xb.at[slab, c, xl, pl.ds(16 * way, 16)], zr.at[slab, way]

    def ring(way, h):
        slab = (z + NZ - h) % NZ if way == 0 else (z + h) % NZ
        place, arrived = ring_place(slab, h + 1, way)
        src = x_in if h == 0 else place
        return rcopy(src, place, zs.at[way, h], arrived, z_up if way == 0 else z_down)

    def ring_got(way, h):
        slab = (z + NZ - h) % NZ if way == 0 else (z + h) % NZ
        got(*ring_place(slab, h, way))

    def x2copy(zz, src=None):
        place = xb.at[zz, c, xl]
        return rcopy(place if src is None else src, place, x2s.at[zz], x2r.at[zz], x_mate)

    def x2_got(zz):
        got(xb.at[zz, c, 1 - xl], x2r.at[zz])

    ring(0, 0).start()
    ring(1, 0).start()
    x2copy(z, x_in).start()

    def c3copy(zz):
        return rcopy(xb.at[zz, c], xb.at[zz, c], c3s.at[zz], c3r.at[zz], core_mate)

    def cot_copy(i, src, b, dev):
        return rcopy(src, cb.at[b], cs.at[i], cr.at[b], dev)

    b_far = y * 2 + 1 - xh
    b_dn = ((y + NY - 1) % NY) * 2 + xh
    b_upfar = ((y + 1) % NY) * 2 + 1 - xh
    cot_sends = [
        cot_copy(0, c_in, row, far_mate),
        cot_copy(1, c_in, row, y_up),
        cot_copy(2, c_in, row, y_down),
        cot_copy(3, cb.at[b_far], b_far, y_up),
        cot_copy(4, cb.at[b_far], b_far, y_down),
        cot_copy(5, cb.at[b_dn], b_dn, y_up),
        cot_copy(6, cb.at[b_upfar], b_upfar, y_down),
    ]
    cot_sends[0].start()

    for one in loads:
        one.wait()
    a_all = a_v[...].reshape(NR * 2 * 16, width)
    aat = mm_nt(a_all, a_all)
    same = lax.broadcasted_iota(jnp.int32, aat.shape, 0) // 16 == lax.broadcasted_iota(jnp.int32, aat.shape, 1) // 16
    gram = jnp.where(same, aat, 0.0)
    gram_hi = gram.astype(BF)
    gram_lo = (gram - gram_hi.astype(F32)).astype(BF)
    for n0, n1 in lane_tiles(cols):
        wt = w_v[:, n0:n1]
        ut = u_v[:, :, n0:n1].reshape(256, n1 - n0)
        val = 2.0 * mm(a_all, wt) + (mm(gram_hi, ut) + mm(gram_lo, ut))
        quad = jnp.sum((ut.astype(F32) * val).reshape(16, 16, n1 - n0), axis=1)
        wf = wt.astype(F32)
        wsq = jnp.sum(jnp.sum((wf * wf).reshape(width // 8, 8, n1 - n0), axis=0), axis=0, keepdims=True)
        nsq = quad + wsq
        for r in range(NR):
            nsend[r, :, n0:n1] = nsq[2 * r:2 * r + 2]
    nrecv[row] = nsend[row]

    def n1copy(o):
        r = (row + o) % NR
        return rcopy(nsend.at[r], nrecv.at[row], n1s.at[o], n1r.at[row], at_row(r))

    for o in range(1, NR):
        n1copy(o).start()
    for one in cot_sends[1:3]:
        one.start()

    def n2copy(o):
        r = (row + o) % NR
        return rcopy(sbuf.at[row], sbuf.at[row], n2s.at[o], n2r.at[row], at_row(r))

    def l1copy(r):
        return rcopy(lsend.at[r], lrecv.at[row], l1s.at[r], l1r.at[row], at_row(r))

    def l2copy(o):
        r = (row + o) % NR
        return rcopy(lowb.at[row], lowb.at[row], l2s.at[o], l2r.at[row], at_row(r))

    def z_of(k):
        return (z + NZ + jnp.where(k % 2 == 1, (k + 1) // 2, -(k // 2))) % NZ

    def b_of(q):
        dy = jnp.where(q >= 6, 2, jnp.where(q % 3 == 2, 3, q % 3))
        dx = jnp.where(q >= 6, q - 6, q // 3)
        return ((y + dy) % NY) * 2 + (xh + dx) % 2

    def pre_slot(dy, xx):
        return jnp.where(dy == 2, 4 + xx, jnp.where(dy == 1, xx, 2 + xx))

    def pre_copy(dy, xx, half):
        slot = pre_slot(dy, xx)
        up = (dy == 1) | ((dy == 2) & (xx == 0))
        yy = jnp.where(up, (y + 1) % NY, (y + NY - 1) % NY)
        part = pl.ds(64 * half, 64)
        return rcopy(
            ps.at[dy, xx, part], rb.at[slot, part], pss.at[slot, half], prs.at[slot, half], at_row(yy * 2 + xh)
        )

    def pre_got(slot, half):
        got(rb.at[slot, pl.ds(64 * half, 64)], prs.at[slot, half])

    def far_copy(half):
        part = pl.ds(64 * half, 64)
        return rcopy(xsb.at[part], xrb.at[part], pxs.at[half], pxr.at[half], far_mate)

    def bccopy(b):
        return rcopy(csend.at[b], crecv.at[b], bcs.at[b], bcr.at[b], core_mate)

    def bxcopy(b):
        return rcopy(xsend.at[b], xrecv.at[b], bxs.at[b], bxr.at[b], x_mate)

    def bzcopy(b):
        return rcopy(zsend.at[b], zrecv.at[z], bzs.at[b], bzr.at[z], at_col(b, xl, c))

    def forward_block(zz):
        xs = jnp.concatenate([xb[zz, 0, 0], xb[zz, 1, 0], xb[zz, 0, 1], xb[zz, 1, 1]], axis=0)
        dy = (zz // 2 + NY - y) % NY
        xx = zz % 2
        for n0, n1 in lane_tiles(cols):
            part = mm(xs, w_v[:, n0:n1])
            pf[dy, xx, :, n0:n1] = part
            ps[dy, xx, :, n0:n1] = part.astype(BF)
        low = mm_nt(a_v[block_tenant(zz)], xs)
        lsend[zz] = low

        @pl.when((dy == 2) | ((dy == 1) & (xx == 1)) | ((dy == 3) & (xx == 0)))
        def _():
            for half in range(2):
                pre_copy(dy, xx, half).start()

        @pl.when(zz != row)
        def _():
            l1copy(zz).start()

        @pl.when(zz == row)
        def _():
            lrecv[row] = low

    def token_scale(b):
        t = block_tenant(b)
        s = sbuf[...]
        number = lax.broadcasted_iota(jnp.int32, s.shape, 0) * 2 + lax.broadcasted_iota(jnp.int32, s.shape, 1)
        return jnp.sum(jnp.sum(jnp.where(number == t, s, 0.0), axis=0), axis=0, keepdims=True)

    def backward_block(b):
        t = block_tenant(b)
        sg = (cb[b].astype(F32) * token_scale(b)).astype(BF)
        sgb[b] = sg
        u = u_v[t]
        a = a_v[t]
        back = mm_nt(sg, jnp.concatenate([u, u], axis=0))
        hi = back.astype(BF).astype(F32)
        lane = lax.broadcasted_iota(jnp.int32, back.shape, 1)
        both = jnp.where(lane < 16, hi, back - hi).astype(BF)
        a2 = jnp.concatenate([a, a], axis=0)
        for n0, n1 in lane_tiles(width):
            part = mm_nt(sg, w_v[n0:n1, :]) + mm(both, a2[:, n0:n1])
            gp[b, :, :, :, n0:n1] = part.reshape(2, 2, 32, n1 - n0)
        csend[b] = gp[b, :, 1 - c].astype(BF)
        bccopy(b).start()

    def step(s, carry):
        for h, at in ((1, 0), (2, 2), (3, 4)):
            @pl.when(s == at)
            def _():
                for way in range(2):
                    ring_got(way, h)
                    ring(way, h).start()
                for zz in ((z + NZ - h) % NZ, (z + h) % NZ):
                    x2copy(zz).start()
                for zz in ((z + NZ - h + 1) % NZ, (z + h - 1) % NZ)[: 1 if h == 1 else 2]:
                    x2_got(zz)
                    c3copy(zz).start()

        @pl.when(s == 6)
        def _():
            ring_got(0, 4)
            ring_got(1, 4)
            x2copy((z + 4) % NZ).start()
            for zz in ((z + NZ - 3) % NZ, (z + 3) % NZ):
                x2_got(zz)
                c3copy(zz).start()

        @pl.when(s == 7)
        def _():
            x2_got((z + 4) % NZ)
            c3copy((z + 4) % NZ).start()

        @pl.when(s == AT_FAR)
        def _():
            got(cb.at[b_far], cr.at[b_far])
            cot_sends[3].start()
            cot_sends[4].start()

        @pl.when(s == AT_DOWN)
        def _():
            got(cb.at[b_dn], cr.at[b_dn])
            cot_sends[5].start()

        @pl.when(s == AT_NORM)
        def _():
            for o in range(1, NR):
                r = (row + o) % NR
                got(nrecv.at[r], n1r.at[r])
            total = jnp.sum(nrecv[...], axis=0)
            m = mag[...]
            number = lax.broadcasted_iota(jnp.int32, m.shape, 0)
            mine = jnp.concatenate(
                [jnp.sum(jnp.where(number == 2 * row + i, m, 0.0), axis=0, keepdims=True) for i in range(2)], axis=0
            )
            sbuf[row] = mine / jnp.sqrt(total + EPS)
            for o in range(1, NR):
                n2copy(o).start()

        @pl.when((s == 1) | ((s >= 3) & (s < NZ + 2)))
        def _():
            zz = z_of(jnp.where(s == 1, 0, s - 2))
            got(xb.at[zz, 1 - c], c3r.at[zz])
            forward_block(zz)

        @pl.when(s == AT_SCALE)
        def _():
            for o in range(1, NR):
                r = (row + o) % NR
                got(sbuf.at[r], n2r.at[r])

        @pl.when(s == AT_UPFAR)
        def _():
            got(cb.at[b_upfar], cr.at[b_upfar])
            cot_sends[6].start()

        @pl.when(s == AT_LOW)
        def _():
            for o in range(1, NR):
                r = (row + o) % NR
                got(lrecv.at[r], l1r.at[r])
            low = jnp.sum(lrecv[...], axis=0)
            lowb[row] = low.astype(BF)
            for o in range(1, NR):
                l2copy(o).start()
            low_mine = low.astype(BF).astype(F32).T.astype(BF)
            u_mine = u_v[block_tenant(row)]
            for n0, n1 in lane_tiles(cols):
                pf[0, xh, :, n0:n1] = pf[0, xh, :, n0:n1] + mm(low_mine, u_mine[:, n0:n1])

        @pl.when((s >= FIRST_BACK) & (s < FIRST_BACK + NR))
        def _():
            q = s - FIRST_BACK
            b = b_of(q)

            @pl.when((q == 1) | (q >= 5))
            def _():
                got(cb.at[b], cr.at[b])

            backward_block(b)

        @pl.when((s >= FIRST_BACK + LAG_X) & (s < FIRST_BACK + LAG_X + NR))
        def _():
            b = b_of(s - FIRST_BACK - LAG_X)
            got(crecv.at[b], bcr.at[b])
            xsend[b] = (gp[b, 1 - xl, c] + crecv[b, 1 - xl].astype(F32)).astype(BF)
            bxcopy(b).start()
            e_own[b] = gp[b, xl, c] + crecv[b, xl].astype(F32)

        @pl.when(s >= FIRST_BACK + LAG_Z)
        def _():
            b = b_of(s - FIRST_BACK - LAG_Z)
            got(xrecv.at[b], bxr.at[b])
            both = e_own[b] + xrecv[b].astype(F32)
            zsend[b] = both.astype(BF)

            @pl.when(b != z)
            def _():
                bzcopy(b).start()

            @pl.when(b == z)
            def _():
                e_own[b] = both

        @pl.when(s == AT_VIA)
        def _():
            for half in range(2):
                rows = pl.ds(64 * half, 64)
                for slot, dy, xx in ((4, 1, 0), (5, 3, 1)):
                    pre_got(slot, half)
                    ps[dy, xx, rows] = (pf[dy, xx, rows] + rb[slot, rows].astype(F32)).astype(BF)
                    pre_copy(dy, xx, half).start()

        return carry

    lax.fori_loop(0, STEPS, step, 0)

    def magnitude_part(b, carry):
        dy = (b // 2 + NY - y) % NY
        part = jnp.sum(cb[b].astype(F32) * pf[dy, b % 2], axis=0, keepdims=True)
        gms[row, b] = part * token_scale(b)
        return carry

    lax.fori_loop(0, NR, magnitude_part, 0)

    def gcopy(o):
        r = (row + o) % NR
        return rcopy(gms.at[row], gms.at[row], gs.at[o], gr.at[row], at_row(r))

    for o in range(1, NR):
        gcopy(o).start()

    xx = 1 - xh
    for half in range(2):
        rows = pl.ds(64 * half, 64)
        pre_got(xx, half)
        pre_got(2 + xx, half)
        xsb[rows] = (pf[0, xx, rows] + rb[xx, rows].astype(F32) + rb[2 + xx, rows].astype(F32)).astype(BF)
        far_copy(half).start()

    for o in range(1, NR):
        r = (row + o) % NR
        got(lowb.at[r], l2r.at[r])
    pieces = []
    for b in range(NR):
        wide = jnp.concatenate([lowb[b].astype(F32)] * 16, axis=0)
        number = lax.broadcasted_iota(jnp.int32, wide.shape, 0) // 16
        pieces.append(jnp.where(number == block_tenant(b), wide, 0.0).astype(BF))
    low_wide = jnp.concatenate(pieces, axis=1)
    for n0, n1 in lane_tiles(cols):
        sg = sgb[:, :, n0:n1].reshape(NR * 128, n1 - n0)
        gb_v[:, :, n0:n1] = mm(low_wide, sg).reshape(16, 16, n1 - n0)
    gb_out = pltpu.make_async_copy(gb_v, gb_ref, gb_sem)
    gb_out.start()

    for o in range(1, NZ):
        zz = (z + o) % NZ
        got(zrecv.at[zz], bzr.at[zz])
    total = e_own[z]
    for o in range(1, NZ):
        total = total + zrecv[(z + o) % NZ].astype(F32)
    gi_ref[...] = total.astype(BF)

    scale_mine = token_scale(row)

    for half in range(2):
        rows = pl.ds(64 * half, 64)
        pre_got(xh, half)
        pre_got(2 + xh, half)
        got(xrb.at[rows], pxr.at[half])
        for n0, n1 in lane_tiles(cols):
            pre = pf[0, xh, rows, n0:n1] + rb[xh, rows, n0:n1].astype(F32) + rb[2 + xh, rows, n0:n1].astype(F32)
            pre = pre + xrb[rows, n0:n1].astype(F32)
            out_ref[rows, n0:n1] = (pre * scale_mine[:, n0:n1]).astype(BF)

    for o in range(1, NR):
        r = (row + o) % NR
        got(gms.at[r], gr.at[r])
    sums = jnp.sum(gms[...], axis=0)
    m = mag[...]
    number = lax.broadcasted_iota(jnp.int32, m.shape, 0)
    acc = jnp.zeros_like(m)
    for b in range(NR):
        acc = acc + jnp.where(number == block_tenant(b), sums[b], 0.0)
    gm_ref[...] = acc / m

    gb_out.wait()
    for o in range(1, NZ):
        sent(nsend.at[0], n1s.at[o])
        sent(sbuf.at[0], n2s.at[o])
        sent(lowb.at[0], l2s.at[o])
        sent(gms.at[0], gs.at[o])
    for k in range(NZ):
        sent(xb.at[k, 0, 0], x2s.at[k])
        sent(xb.at[k, 0], c3s.at[k])
        sent(csend.at[k], bcs.at[k])
        sent(xsend.at[k], bxs.at[k])

        @pl.when(k != z)
        def _():
            sent(zsend.at[k], bzs.at[k])

        @pl.when(k != row)
        def _():
            sent(lsend.at[k], l1s.at[k])
    for i in range(7):
        sent(c_in, cs.at[i])
    for half in range(2):
        rows = pl.ds(64 * half, 64)
        for slot in range(6):
            sent(rb.at[slot, rows], pss.at[slot, half])
        sent(xsb.at[rows], pxs.at[half])
    for way in range(2):
        for h in range(4):
            sent(x_in if h < 3 else x_in.at[pl.ds(0, 16)], zs.at[way, h])


def hand_over(*refs):
    held, into, out = refs[8:12], refs[12], refs[13]
    ins = [pltpu.make_async_copy(refs[i], held[i], into.at[i]) for i in range(4)]
    outs = [pltpu.make_async_copy(held[i], refs[4 + i], out.at[i]) for i in range(4)]
    for one in ins:
        one.start()
    for i in range(4):
        ins[i].wait()
        outs[i].start()
    for one in outs:
        one.wait()


def shards(inputs, weight, adapter_down_factors, adapter_up_factors, magnitude, cotangent, tenant):
    width, cols = weight.shape
    tokens, rows = inputs.shape[0], cotangent.shape[0]
    any_, vmem = pl.BlockSpec(memory_space=pl.ANY), pl.BlockSpec(memory_space=pltpu.VMEM)
    dma = pltpu.SemaphoreType.DMA
    V = pltpu.VMEM
    parts = pl.pallas_call(
        kernel,
        out_shape=(
            jax.ShapeDtypeStruct((rows, cols), BF),
            jax.ShapeDtypeStruct((tokens, width), BF),
            jax.ShapeDtypeStruct((16, 16, cols), F32),
            jax.ShapeDtypeStruct((16, cols), F32),
        ),
        in_specs=[pl.BlockSpec(memory_space=pltpu.SMEM), any_, any_, any_, any_, vmem, any_],
        out_specs=(vmem, vmem, any_, vmem),
        scratch_shapes=[
            V((width, cols), BF), V((16, 16, width), BF), V((16, 16, cols), BF),
            V((NZ, 2, 2, tokens, width), BF), V((NR, rows, cols), BF), V((NR, rows, cols), BF),
            V((16, 16, cols), F32),
            V((NR, 2, cols), F32), V((NR, 2, cols), F32), V((NR, 2, cols), F32),
            V((NR, 16, rows), F32), V((NR, 16, rows), F32), V((NR, 16, rows), BF),
            V((NY, 2, rows, cols), F32), V((NY, 2, rows, cols), BF), V((6, rows, cols), BF),
            V((rows, cols), BF), V((rows, cols), BF),
            V((NR, 2, 2, tokens, width), F32), V((NR, 2, tokens, width), BF), V((NR, 2, tokens, width), BF),
            V((NR, tokens, width), F32),
            V((NR, tokens, width), BF), V((NR, tokens, width), BF),
            V((NR, tokens, width), BF), V((NR, tokens, width), BF),
            V((NR, NR, 1, cols), F32),
            dma((5,)), dma,
            dma((2, 4)), dma((8, 2)), dma((8,)), dma((8,)), dma((8,)), dma((8,)),
            dma((7,)), dma((8,)),
            dma((8,)), dma((8,)), dma((8,)), dma((8,)), dma((8,)), dma((8,)), dma((8,)), dma((8,)), dma((8,)), dma((8,)),
            dma((6, 2)), dma((6, 2)), dma((2,)), dma((2,)),
            dma((8,)), dma((8,)), dma((8,)), dma((8,)), dma((8,)), dma((8,)),
        ],
        compiler_params=pltpu.CompilerParams(
            collective_id=0, has_side_effects=True, vmem_limit_bytes=56 << 20
        ),
        cost_estimate=pl.CostEstimate(flops=6 * 10**9, bytes_accessed=8 * 10**6, transcendentals=10**5),
        name="adapter_step",
    )(tenant, inputs, weight, adapter_down_factors, adapter_up_factors, magnitude, cotangent)
    return pl.pallas_call(
        hand_over,
        out_shape=[jax.ShapeDtypeStruct(p.shape, p.dtype) for p in parts],
        in_specs=[any_] * 4,
        out_specs=[any_] * 4,
        scratch_shapes=[V(p.shape, p.dtype) for p in parts] + [dma((4,)), dma((4,))],
        name="hand_over",
    )(*parts)


def solution(mesh):
    return jax.shard_map(
        shards,
        mesh=mesh,
        in_specs=(
            P("col", "row"),
            P("row", "col"),
            P(None, None, "row"),
            P(None, None, "col"),
            P(None, "col"),
            P("row", "col"),
            P(),
        ),
        out_specs=(P("row", "col"), P("col", "row"), P(None, None, "col"), P(None, "col")),
        check_vma=False,
    )
```
